512 devices in a mesh: dp: 32 (over z, x), tensor: 16 (over y, core).
Axes of the slice: x: 4, y: 8, z: 8, core: 2. Of those that a mesh axis runs over, the one named last changes fastest.
Arguments:
- reward: float32 [384], P('dp'), may hold values from 0 to 4
- group_id: int32 [384], P('dp'), may hold values from 0 to 23, as said below
- keep: int32 [384], P('dp'), may hold values from 0 to 1, as said below
- dest: int32 [384], P('dp'), may hold values from -1 to 255, as said below
- doc_len: int32 [32, 8], P('dp'), may hold values from 1 to 512, 2048 in all within a row
- query: bfloat16 [65536, 2048], P(('dp', 'tensor')), may hold values from -6 to 6
- key: bfloat16 [65536, 1024], P(('dp', 'tensor')), may hold values from -6 to 6
- value: bfloat16 [65536, 1024], P(('dp', 'tensor')), may hold values from -6 to 6
- grad_out: bfloat16 [65536, 2048], P(('dp', 'tensor')), may hold values from -6 to 6
Outputs:
- grad_query: bfloat16 [65536, 2048], P(('dp', 'tensor'))
- grad_key: bfloat16 [65536, 1024], P(('dp', 'tensor'))
- grad_value: bfloat16 [65536, 1024], P(('dp', 'tensor'))
The draws below stay inside these ranges and needn't reach their ends.
Inputs may be any that keep to these rules, and one draw needn't show every extreme that they name: `group_id`: every prompt has exactly 16 rollouts. `keep`: exactly 8 of the 12 rollouts of each index of dp are kept. `dest`: kept rollouts take distinct slots and fill all of them; dropped ones have -1. `doc_len`: each row sums to 2048; its longest document has exactly 512 tokens.
All inputs are finite; a program needn't handle non-finite values.
Results may differ from the reference program's by a relative error of at most 0.0059.
Values may be sent and summed in bfloat16 or wider, within the bound.
A program may use at most 64 MiB of HBM per device.

```python
import math
import jax
import jax.numpy as jnp
import numpy as np
from jax import lax

HQ = 16
KVH = 8
HD = 128
TOK_DEV = 128
SLOTS = 8
ROLL_DEV = 12
GROUP = 16
REACH = 4
GROUP_TOK = 2048
MOST = 512
TOKENS = 65536
ROLLS = 384
NGROUPS = 24
N_DP = 32
N_TENSOR = 16


def kept_layout(base_key):
    device_count = ROLLS // ROLL_DEV
    device_keys = jax.random.split(base_key, device_count)
    rank_rows = jax.vmap(lambda single: jax.random.permutation(single, ROLL_DEV))(device_keys)
    return (rank_rows < SLOTS).astype(jnp.int32).reshape(ROLLS)


def draw_keep(key, part):
    return kept_layout(key)


def draw_dest(key, part):
    kept_flags = kept_layout(key)
    key = jax.random.fold_in(key, 7)
    slot_order = jax.random.permutation(key, SLOTS * (ROLLS // ROLL_DEV)).astype(jnp.int32)
    position = jnp.maximum(jnp.cumsum(kept_flags) - 1, 0).astype(jnp.int32)
    return jnp.where(kept_flags > 0, slot_order[position], -1).astype(jnp.int32)


def draw_group_id(key, part):
    key = jax.random.fold_in(key, 3)
    return (jax.random.permutation(key, ROLLS) // GROUP).astype(jnp.int32)


def block_levels(key, shape, cuts, low, top_value):
    def one(axis_at, shards_of):
        draws = jax.random.uniform(jax.random.fold_in(jax.random.fold_in(key, 6), axis_at), (shards_of,), jnp.float32, low / len(cuts), top_value / len(cuts))
        return jnp.repeat(jnp.exp(draws), shape[axis_at] // shards_of).reshape((-1,) + (1,) * (len(shape) - axis_at - 1))

    factor_of = one(*cuts[0])
    for cut in cuts[1:]:
        factor_of = factor_of * one(*cut)
    return factor_of


def length_profile(number_of, total, most, slope):
    portions = [(1 << 20) // math.isqrt(grade ** slope) + 1 for grade in range(2, number_of + 1)]
    rest, holding = total - most - (number_of - 1), [1] * (number_of - 1)
    while rest > 0:
        movable = [i for i in range(number_of - 1) if holding[i] < most]
        whole, remaining = sum([portions[i] for i in movable]), rest
        for i in movable:
            addition = min(most - holding[i], max(1, remaining * portions[i] // whole), rest)
            holding[i] = holding[i] + addition
            rest = rest - addition
    return np.array([most] + holding)


def uneven(own_key, count, total, limit, slope):
    if count == 2:
        one = jax.random.randint(own_key, (), max(1, total - limit), min(limit, total - 1) + 1)
        return jnp.stack([one, total - one])
    lengths = jnp.asarray(length_profile(count, total, limit, slope), jnp.int32)
    couples = (count - 1) // 2
    giver, taker = lengths[1:1 + 2 * couples:2], lengths[2:2 + 2 * couples:2]
    room = jnp.minimum(giver - 1, limit - taker)
    moved = jax.random.randint(jax.random.fold_in(own_key, 1), (couples,), 0, 1 << 20) % (room + 1)
    lengths = lengths.at[1:1 + 2 * couples:2].set(giver - moved).at[2:2 + 2 * couples:2].set(taker + moved)
    return lengths[jax.random.permutation(jax.random.fold_in(own_key, 2), count)]


def scatter_about(stream_key, dims, scale, most, cuts=(), kind=jnp.bfloat16):
    gain = block_levels(stream_key, dims, cuts, -0.22, 0.18) if cuts else 1.0
    entries = jax.random.normal(stream_key, dims, jnp.float32) * scale * gain
    return jnp.minimum(jnp.maximum(entries, -most), most).astype(kind)


def setup_inputs(seed: int = 0) -> dict:
    seeds = jax.random.split(jax.random.key(seed), 10)
    reward = jnp.clip(4.0 * jax.random.uniform(seeds[0], (ROLLS,), jnp.float32) ** block_levels(seeds[0], (ROLLS,), ((0, 32),), -0.2, 0.2), 0.0, 4.0)
    group_id = draw_group_id(jax.random.fold_in(seeds[9], 71), 0)
    keep = draw_keep(jax.random.fold_in(seeds[9], 71), 0)
    dest = draw_dest(jax.random.fold_in(seeds[9], 71), 0)
    doc_len = jax.vmap(lambda own: uneven(own, SLOTS, GROUP_TOK, MOST, 2))(jax.random.split(seeds[4], N_DP)).reshape((N_DP, SLOTS)).astype(jnp.int32)
    query = scatter_about(seeds[5], (TOKENS, HQ * HD), 1.0, 6.0, ((0, 512),))
    key = scatter_about(seeds[6], (TOKENS, KVH * HD), 1.0, 6.0, ((0, 512),))
    value = scatter_about(seeds[7], (TOKENS, KVH * HD), 1.0, 6.0, ((0, 512),))
    grad_out = scatter_about(seeds[8], (TOKENS, HQ * HD), 1.0, 6.0, ((0, 512),))
    return dict(reward=reward, group_id=group_id, keep=keep, dest=dest, doc_len=doc_len, query=query, key=key, value=value, grad_out=grad_out)


softcap = 50.0
inv_scale = 1.0 / 12.0

def group_table(group_id, groups_all):
    return (group_id[:, None] == jnp.arange(groups_all, dtype=jnp.int32)[None, :]).astype(jnp.float32)

def group_advantage(reward, group_hot, kept_rows, member_count, reward_sum, square):
    members = jnp.maximum(member_count, 1.0)
    average = reward_sum / members
    spread = jnp.sqrt(jnp.maximum(square / members - average * average, 0.0))
    divisor = jnp.maximum(spread, 1.0)
    row_mean = lax.optimization_barrier(jnp.sum(group_hot * average[None, :], axis=1))
    row_divisor = lax.optimization_barrier(jnp.sum(group_hot * divisor[None, :], axis=1))
    return kept_rows * (reward - row_mean) / row_divisor

def segment_of(positions, doc_ends):
    return lax.optimization_barrier(jnp.sum((positions[:, None] >= doc_ends[None, :]).astype(jnp.int32), axis=1))

def multiply(form, left, right):
    return jnp.einsum(form, left.astype(jnp.float32), right.astype(jnp.float32), precision=lax.Precision.HIGHEST)

def block_terms(query_block, key_window, value_window, grad_block, query_pos, key_pos, query_seg, key_seg):
    logits = multiply('qgrd,kgd->grqk', query_block, key_window) * inv_scale
    capped = jnp.tanh(logits / softcap)
    allowed = (key_seg[None, :] == query_seg[:, None]) & (key_pos[None, :] <= query_pos[:, None]) & (key_pos[None, :] >= 0)
    exponent = jnp.where(allowed[None, None], jnp.exp(softcap * capped), 0.0)
    probs = exponent / lax.optimization_barrier(jnp.sum(exponent, axis=-1, keepdims=True))
    prob_grad = multiply('qgrd,kgd->grqk', grad_block, value_window)
    row_delta = lax.optimization_barrier(jnp.sum(probs * prob_grad, axis=-1, keepdims=True))
    logit_grad = (probs * (prob_grad - row_delta) * (1.0 - capped * capped) * inv_scale).astype(jnp.bfloat16)
    probs_low = probs.astype(jnp.bfloat16)
    grad_q = multiply('grqk,kgd->qgrd', logit_grad, key_window)
    grad_k = multiply('grqk,qgrd->kgd', logit_grad, query_block)
    grad_v = multiply('grqk,qgrd->kgd', probs_low, grad_block)
    return (grad_q, grad_k, grad_v)

def row_backward(row_data):
    query_row, key_row, value_row, grad_row, seg_row = row_data
    margin = REACH * TOK_DEV
    width = margin + TOK_DEV
    heads_query = query_row.reshape(GROUP_TOK, KVH, HQ // KVH, HD)
    heads_grad = grad_row.reshape(GROUP_TOK, KVH, HQ // KVH, HD)
    front = jnp.zeros((margin, KVH * HD), jnp.bfloat16)
    keys_pad = jnp.concatenate([front, key_row], axis=0).reshape(GROUP_TOK + margin, KVH, HD)
    values_pad = jnp.concatenate([front, value_row], axis=0).reshape(GROUP_TOK + margin, KVH, HD)
    seg_pad = jnp.concatenate([jnp.full((margin,), -1, jnp.int32), seg_row.astype(jnp.int32)])
    pos_pad = jnp.arange(GROUP_TOK + margin, dtype=jnp.int32) - margin

    def advance(carry, block):
        key_acc, value_acc = carry
        start = (block * TOK_DEV).astype(jnp.int32)
        query_block = lax.dynamic_slice_in_dim(heads_query, start, TOK_DEV, 0)
        grad_block = lax.dynamic_slice_in_dim(heads_grad, start, TOK_DEV, 0)
        query_pos = lax.dynamic_slice_in_dim(pos_pad, start + margin, TOK_DEV, 0)
        query_seg = lax.dynamic_slice_in_dim(seg_pad, start + margin, TOK_DEV, 0)
        key_window = lax.dynamic_slice_in_dim(keys_pad, start, width, 0)
        value_window = lax.dynamic_slice_in_dim(values_pad, start, width, 0)
        key_pos = lax.dynamic_slice_in_dim(pos_pad, start, width, 0)
        key_seg = lax.dynamic_slice_in_dim(seg_pad, start, width, 0)
        grad_q, grad_k, grad_v = block_terms(query_block, key_window, value_window, grad_block, query_pos, key_pos, query_seg, key_seg)
        key_acc = lax.dynamic_update_slice_in_dim(key_acc, lax.dynamic_slice_in_dim(key_acc, start, width, 0) + grad_k, start, 0)
        value_acc = lax.dynamic_update_slice_in_dim(value_acc, lax.dynamic_slice_in_dim(value_acc, start, width, 0) + grad_v, start, 0)
        return ((key_acc, value_acc), grad_q.astype(jnp.bfloat16))
    zeros = jnp.zeros((GROUP_TOK + margin, KVH, HD), jnp.float32)
    (key_acc, value_acc), grad_q = lax.scan(advance, (zeros, zeros), jnp.arange(N_TENSOR, dtype=jnp.int32))
    grad_query = grad_q.reshape(GROUP_TOK, HQ * HD)
    grad_key = key_acc[margin:].astype(jnp.bfloat16).reshape(GROUP_TOK, KVH * HD)
    grad_value = value_acc[margin:].astype(jnp.bfloat16).reshape(GROUP_TOK, KVH * HD)
    return (grad_query, grad_key, grad_value)

def reference(reward, group_id, keep, dest, doc_len, query, key, value, grad_out):
    kept_rows = keep.astype(jnp.float32)
    group_hot = group_table(group_id, NGROUPS)
    member_count = lax.optimization_barrier(jnp.sum(group_hot * kept_rows[:, None], axis=0))
    reward_sum = lax.optimization_barrier(jnp.sum(group_hot * (kept_rows * reward)[:, None], axis=0))
    square = lax.optimization_barrier(jnp.sum(group_hot * (kept_rows * reward * reward)[:, None], axis=0))
    advantage = group_advantage(reward, group_hot, kept_rows, member_count, reward_sum, square)
    placed = (dest[:, None] == jnp.arange(N_DP * SLOTS, dtype=jnp.int32)[None, :]).astype(jnp.float32)
    slot_adv = lax.optimization_barrier(jnp.sum(placed * advantage[:, None], axis=0)).reshape(N_DP, SLOTS)
    doc_ends = jnp.cumsum(doc_len, axis=1).astype(jnp.int32)
    positions = jnp.arange(GROUP_TOK, dtype=jnp.int32)
    segments = jax.vmap(lambda row_ends: segment_of(positions, row_ends))(doc_ends)
    slot_hit = (segments[:, :, None] == jnp.arange(SLOTS, dtype=jnp.int32)[None, None, :]).astype(jnp.float32)
    weight = lax.optimization_barrier(jnp.sum(slot_hit * slot_adv[:, None, :], axis=2)).reshape(TOKENS, 1)
    scaled = (weight * grad_out.astype(jnp.float32)).astype(jnp.bfloat16)
    row_data = (query.reshape(N_DP, GROUP_TOK, HQ * HD), key.reshape(N_DP, GROUP_TOK, KVH * HD), value.reshape(N_DP, GROUP_TOK, KVH * HD), scaled.reshape(N_DP, GROUP_TOK, HQ * HD), segments)
    grad_query, grad_key, grad_value = lax.map(row_backward, row_data)
    return (grad_query.reshape(TOKENS, HQ * HD), grad_key.reshape(TOKENS, KVH * HD), grad_value.reshape(TOKENS, KVH * HD))
```

```python
import math

import jax
import jax.numpy as jnp
from jax import lax
from jax.experimental import pallas as pl
from jax.experimental.pallas import tpu as pltpu
from jax.sharding import PartitionSpec as P

HD = 128
TOK = 128
CHIP = 2 * TOK
SLOTS = 8
GROUP = 16
ROLL = 12
HEADS = 4
MESH = pl.DeviceIdType.MESH
F32 = jnp.float32
BF16 = jnp.bfloat16

softcap = 50.0
to_capped = 1.0 / (12.0 * softcap)
to_exponent = softcap * math.log2(math.e)


def head_cols(index, width=1):
    return pl.ds(pl.multiple_of(index * HD, HD), width * HD)


def rows_of(start):
    return pl.ds(pl.multiple_of(start, TOK), TOK)


def advantage_table(all_ref, groups, row):
    planes = all_ref.shape[0] * all_ref.shape[1]

    def field(n):
        return jnp.concatenate(
            [all_ref[i // all_ref.shape[1], i % all_ref.shape[1], n : n + 1, :] for i in range(planes)], axis=0
        )

    reward, group, keep, dest = field(0), field(1), field(2), field(3)
    counts, sums, squares = [], [], []
    for g in range(groups):
        member = jnp.where(group == float(g), keep, 0.0)
        counts.append(jnp.sum(member, axis=0, keepdims=True))
        sums.append(jnp.sum(member * reward, axis=0, keepdims=True))
        squares.append(jnp.sum(member * reward * reward, axis=0, keepdims=True))

    def total(parts):
        return jnp.sum(jnp.concatenate(parts, axis=0), axis=1, keepdims=True)

    members = jnp.maximum(total(counts), 1.0)
    average = total(sums) / members
    spread = jnp.sqrt(jnp.maximum(total(squares) / members - average * average, 0.0))
    divisor = jnp.maximum(spread, 1.0)
    row_mean = jnp.zeros_like(reward)
    row_divisor = jnp.zeros_like(reward)
    for g in range(groups):
        own = group == float(g)
        row_mean = jnp.where(own, average[g : g + 1, :], row_mean)
        row_divisor = jnp.where(own, divisor[g : g + 1, :], row_divisor)
    row_divisor = jnp.maximum(row_divisor, 1.0)
    advantage = keep * (reward - row_mean) / row_divisor
    slots = []
    for s in range(SLOTS):
        wanted = (row * SLOTS + s).astype(F32)
        slots.append(jnp.sum(jnp.where(dest == wanted, advantage, 0.0), axis=0, keepdims=True))
    return total(slots)


def kernel(
    dp_x,
    reward_ref,
    group_ref,
    keep_ref,
    dest_ref,
    doc_ref,
    q_hbm,
    k_hbm,
    v_hbm,
    g_hbm,
    dq_hbm,
    dk_hbm,
    dv_hbm,
    kv,
    qs,
    gs,
    mask,
    weight,
    rolls,
    near,
    mine,
    far_out,
    far_in,
    near_out,
    near_in,
    side_out,
    side_in,
    dq_own,
    dq_side,
    done,
    own_ss,
    own_rs,
    relay_ss,
    relay_rs,
    far_ss,
    far_rs,
    near_ss,
    near_rs,
    side_ss,
    side_rs,
    pair_ss,
    pair_rs,
    dq_ss,
    dq_rs,
    load_s,
    store_s,
    out_s,
    x_ss,
    x_rs,
    z_ss,
    z_rs,
):
    dp = lax.axis_index("dp")
    ti = lax.axis_index("tensor")
    chips = lax.axis_size("tensor") // 2
    dp_z = lax.axis_size("dp") // dp_x
    chip, core = ti // 2, ti % 2
    other = 1 - core
    up, down = (chip + 1) % chips, (chip + chips - 1) % chips
    px, pz = dp % dp_x, dp // dp_x

    def at(c, k):
        return (dp, 2 * c + k)

    sibling = at(chip, other)
    x_peers = [(pz * dp_x + (px + i) % dp_x, ti) for i in range(1, dp_x)]
    z_peers = [(((pz + i) % dp_z) * dp_x + px, ti) for i in range(1, dp_z)]

    def remote(src, dst, ss, rs, device):
        return pltpu.make_async_remote_copy(
            src_ref=src, dst_ref=dst, send_sem=ss, recv_sem=rs, device_id=device, device_id_type=MESH
        )

    barrier = pltpu.get_barrier_semaphore()
    partners = [sibling, at(up, 0), at(up, 1), at(down, 0), at(down, 1)] + x_peers + z_peers
    for device in partners:
        pl.semaphore_signal(barrier, inc=1, device_id=device, device_id_type=MESH)

    half = 2 * HEADS * HD
    own_half = pl.ds(pl.multiple_of(core * half, half), half)
    side_half = pl.ds(pl.multiple_of(other * half, half), half)
    own_kv = pl.ds(pl.multiple_of(core * (half // 2), half // 2), half // 2)
    side_kv = pl.ds(pl.multiple_of(other * (half // 2), half // 2), half // 2)
    own_rows = rows_of(2 * CHIP + core * TOK)
    side_rows = rows_of(2 * CHIP + other * TOK)
    loads = [
        pltpu.make_async_copy(k_hbm.at[:, own_kv], kv.at[0, own_rows], load_s.at[0]),
        pltpu.make_async_copy(v_hbm.at[:, own_kv], kv.at[1, own_rows], load_s.at[1]),
        pltpu.make_async_copy(q_hbm.at[:, own_half], qs.at[core], load_s.at[2]),
        pltpu.make_async_copy(g_hbm.at[:, own_half], gs.at[core], load_s.at[3]),
    ]
    for copy in loads:
        copy.start()

    lane = lax.broadcasted_iota(jnp.int32, (8, 128), 1)
    sub = lax.broadcasted_iota(jnp.int32, (8, 128), 0)
    tile = jnp.where((sub == 1) | (sub == 3), -1.0, 0.0) + jnp.zeros((8, 128), F32)
    rolls[pz, px] = tile
    rolls[pz, px, 0:1, 0:ROLL] = reward_ref[...]
    rolls[pz, px, 1:2, 0:ROLL] = group_ref[...].astype(F32)
    rolls[pz, px, 2:3, 0:ROLL] = keep_ref[...].astype(F32)
    rolls[pz, px, 3:4, 0:ROLL] = dest_ref[...].astype(F32)

    pl.semaphore_wait(barrier, len(partners))

    def own_copy(h, i, k):
        src = (k_hbm, v_hbm)[i]
        return remote(
            src.at[:, head_cols(HEADS * k + h)],
            kv.at[i, rows_of(CHIP + core * TOK), head_cols(h)],
            own_ss.at[h, i, k],
            own_rs.at[h, i, core],
            at(up, k),
        )

    def own_arrival(h, i, k):
        dst = kv.at[i, rows_of(CHIP + k * TOK), head_cols(h)]
        return remote(dst, dst, own_ss.at[h, i, k], own_rs.at[h, i, k], at(down, k))

    def relay_copy(h, i):
        return remote(
            kv.at[i, pl.ds(CHIP, CHIP), head_cols(h)],
            kv.at[i, pl.ds(0, CHIP), head_cols(h)],
            relay_ss.at[h, i],
            relay_rs.at[h, i],
            at(up, core),
        )

    def far_copy(h, i):
        return remote(far_out.at[h, i], far_in.at[h, i], far_ss.at[h, i], far_rs.at[h, i], at(down, core))

    def near_copy(h, i, k):
        return remote(
            near_out.at[h, i, pl.ds(k * TOK, TOK)],
            near_in.at[h, i, core],
            near_ss.at[h, i, k],
            near_rs.at[h, i, core],
            at(down, k),
        )

    def near_arrival(h, i, k):
        dst = near_in.at[h, i, k]
        return remote(dst, dst, near_ss.at[h, i, k], near_rs.at[h, i, k], at(up, k))

    def side_copy(h, i):
        return remote(side_out.at[h, i], side_in.at[h, i], side_ss.at[h, i], side_rs.at[h, i], sibling)

    def dq_copy(h):
        return remote(
            dq_side.at[:, head_cols(2 * h, 2)],
            dq_hbm.at[:, head_cols(2 * HEADS * core + 2 * h, 2)],
            dq_ss.at[h],
            dq_rs.at[h],
            sibling,
        )

    def dq_arrival(h):
        dst = dq_hbm.at[:, head_cols(2 * HEADS * other + 2 * h, 2)]
        return remote(dst, dst, dq_ss.at[h], dq_rs.at[h], sibling)

    def dq_store(h):
        return pltpu.make_async_copy(
            dq_own.at[:, head_cols(2 * h, 2)],
            dq_hbm.at[:, head_cols(2 * HEADS * core + 2 * h, 2)],
            store_s.at[h],
        )

    def out_store(h, i, k):
        return pltpu.make_async_copy(
            done.at[i, :, head_cols(HEADS * k + h)],
            (dk_hbm, dv_hbm)[i].at[:, head_cols(HEADS * k + h)],
            out_s.at[h, i, k],
        )

    def start_own(h):
        for i in range(2):
            for k in range(2):
                own_copy(h, i, k).start()

    def pass_on(h):
        for i in range(2):
            for k in range(2):
                own_arrival(h, i, k).wait_recv()
            relay_copy(h, i).start()

    start_own(0)
    x_copies = [
        remote(rolls.at[pz, px], rolls.at[pz, px], x_ss.at[i], x_rs.at[i], device) for i, device in enumerate(x_peers)
    ]
    for copy in x_copies:
        copy.start()
    pair_copies = [
        remote(k_hbm.at[:, side_kv], kv.at[0, own_rows], pair_ss.at[0], pair_rs.at[0], sibling),
        remote(v_hbm.at[:, side_kv], kv.at[1, own_rows], pair_ss.at[1], pair_rs.at[1], sibling),
        remote(q_hbm.at[:, side_half], qs.at[core], pair_ss.at[2], pair_rs.at[2], sibling),
        remote(g_hbm.at[:, side_half], gs.at[core], pair_ss.at[3], pair_rs.at[3], sibling),
    ]
    pair_arrivals = [
        remote(k_hbm.at[:, side_kv], kv.at[0, side_rows], pair_ss.at[0], pair_rs.at[0], sibling),
        remote(v_hbm.at[:, side_kv], kv.at[1, side_rows], pair_ss.at[1], pair_rs.at[1], sibling),
        remote(q_hbm.at[:, side_half], qs.at[other], pair_ss.at[2], pair_rs.at[2], sibling),
        remote(g_hbm.at[:, side_half], gs.at[other], pair_ss.at[3], pair_rs.at[3], sibling),
    ]
    for copy in pair_copies:
        copy.start()
    start_own(1)

    ends = []
    for s in range(SLOTS):
        ends.append(doc_ref[0, s] + (ends[-1] if s else 0))
    for b in range(2):
        query_pos = chip * CHIP + b * TOK + lax.broadcasted_iota(jnp.int32, (1, TOK), 1)
        first = jnp.zeros_like(query_pos)
        for s in range(SLOTS - 1):
            first = jnp.where(query_pos >= ends[s], ends[s], first)
        key_pos = (chip - 2) * CHIP + b * TOK + lax.broadcasted_iota(jnp.int32, (5 * TOK, TOK), 0)
        mask[b] = jnp.where((key_pos <= query_pos) & (key_pos >= first), 1.0, 0.0)

    for i in range(1, dp_x):
        sender = (px + dp_x - i) % dp_x
        arrived = rolls.at[pz, sender]
        remote(arrived, arrived, x_ss.at[i - 1], x_rs.at[i - 1], (pz * dp_x + sender, ti)).wait_recv()
    z_copies = [remote(rolls.at[pz], rolls.at[pz], z_ss.at[i], z_rs.at[i], device) for i, device in enumerate(z_peers)]
    for copy in z_copies:
        copy.start()

    pass_on(0)
    start_own(2)

    for i in range(1, dp_z):
        sender = (pz + dp_z - i) % dp_z
        arrived = rolls.at[sender]
        remote(arrived, arrived, z_ss.at[i - 1], z_rs.at[i - 1], (sender * dp_x + px, ti)).wait_recv()
    groups = lax.axis_size("dp") * ROLL // GROUP
    table = advantage_table(rolls, groups, dp)
    token = chip * CHIP + lax.broadcasted_iota(jnp.int32, (CHIP, HD), 0)
    factor = jnp.zeros((CHIP, HD), F32) + table[0:1, :]
    for s in range(1, SLOTS):
        factor = jnp.where(token >= ends[s - 1], table[s : s + 1, :], factor)
    weight[0] = factor
    weight[1] = factor * (1.0 / 12.0)

    for copy in loads:
        copy.wait()
    for copy in pair_arrivals:
        copy.wait_recv()

    def stacked(ref, b, h):
        return jnp.concatenate([ref[b, :, head_cols(2 * h)], ref[b, :, head_cols(2 * h + 1)]], axis=0)

    def dot(a, b, dims):
        return lax.dot_general(a, b, (dims, ((), ())), preferred_element_type=F32)

    def terms(h, b):
        window = pl.ds(b * TOK, 5 * TOK)
        keys = kv[0, window, head_cols(h)]
        values = kv[1, window, head_cols(h)]
        query, grad = stacked(qs, b, h), stacked(gs, b, h)
        allowed = mask[b]
        capped = jnp.tanh(dot(keys, query, ((1,), (1,))) * to_capped)
        weights = jnp.exp2(capped * to_exponent) * jnp.concatenate([allowed, allowed], axis=1)
        prob_grad = dot(values, grad, ((1,), (1,)))
        inverse = 1.0 / jnp.sum(weights, axis=0, keepdims=True)
        delta = jnp.sum(weights * prob_grad, axis=0, keepdims=True) * inverse
        probs = weights * inverse
        logit_grad = (probs * (prob_grad - delta) * (1.0 - capped * capped)).astype(BF16)
        dv = dot(probs.astype(BF16), grad, ((1,), (0,)))
        dk = dot(logit_grad, query, ((1,), (0,)))
        dq = dot(logit_grad, keys, ((0,), (0,)))
        return dk, dv, dq

    def work(h):
        first, second = terms(h, 0), terms(h, 1)
        for i in range(2):
            a, b = first[i], second[i]
            far_out[h, i, 0:TOK] = a[0:TOK].astype(BF16)
            far_out[h, i, TOK:CHIP] = (a[TOK:CHIP] + b[0:TOK]).astype(BF16)
        for i in range(2):
            far_copy(h, i).start()
        for i in range(2):
            a, b = first[i], second[i]
            near[h, i] = a[CHIP : 2 * CHIP] + b[TOK : TOK + CHIP]
            own_part = (a[4 * TOK : 5 * TOK] + b[3 * TOK : 4 * TOK], b[4 * TOK : 5 * TOK])
            mine[h, i] = jnp.where(core == 0, own_part[0], own_part[1])
            side_out[h, i] = jnp.where(core == 0, own_part[1], own_part[0]).astype(BF16)
            side_copy(h, i).start()
        for b, part in ((0, first[2]), (1, second[2])):
            scale = weight[1, b * TOK : (b + 1) * TOK]
            for r in range(2):
                piece = (part[r * TOK : (r + 1) * TOK] * scale).astype(BF16)

                @pl.when(core == b)
                def _():
                    dq_own[:, head_cols(2 * h + r)] = piece

                @pl.when(core != b)
                def _():
                    dq_side[:, head_cols(2 * h + r)] = piece

        dq_store(h).start()
        dq_copy(h).start()

    def pass_back(h):
        for i in range(2):
            far_copy(h, i).wait_recv()
            near_out[h, i] = (near[h, i] + far_in[h, i].astype(F32)).astype(BF16)
            for k in range(2):
                near_copy(h, i, k).start()

    def finish(h):
        for i in range(2):
            scale = weight[1 - i, rows_of(core * TOK)]
            side_copy(h, i).wait_recv()
            for k in range(2):
                near_arrival(h, i, k).wait_recv()
            a = mine[h, i] + near_in[h, i, core].astype(F32)
            b = side_in[h, i].astype(F32) + near_in[h, i, other].astype(F32)
            done[i, :, head_cols(HEADS * core + h)] = (a * scale).astype(BF16)
            done[i, :, head_cols(HEADS * other + h)] = (b * scale).astype(BF16)
            for k in range(2):
                out_store(h, i, k).start()

    pass_on(1)
    start_own(3)

    def turn(h, carry):
        for i in range(2):
            relay_copy(h, i).wait_recv()
        work(h)

        @pl.when(h < HEADS - 2)
        def _():
            pass_on(h + 2)

        @pl.when(h > 0)
        def _():
            finish(h - 1)

        pass_back(h)
        return carry

    lax.fori_loop(0, HEADS, turn, 0)
    finish(HEADS - 1)

    for copy in x_copies + z_copies + pair_copies:
        copy.wait_send()

    def settle(h, carry):
        for i in range(2):
            for k in range(2):
                own_copy(h, i, k).wait_send()
                near_copy(h, i, k).wait_send()
                out_store(h, i, k).wait()
            relay_copy(h, i).wait_send()
            far_copy(h, i).wait_send()
            side_copy(h, i).wait_send()
        dq_store(h).wait()
        dq_copy(h).wait_send()
        dq_arrival(h).wait_recv()
        return carry

    lax.fori_loop(0, HEADS, settle, 0)


def body(reward, group_id, keep, dest, doc_len, query, key, value, grad_out):
    dp_size = lax.axis_size("dp")
    dp_x = 4 if dp_size % 32 == 0 else 2
    dp_z = dp_size // dp_x
    vmem = pl.BlockSpec(memory_space=pltpu.VMEM)
    smem = pl.BlockSpec(memory_space=pltpu.SMEM)
    hbm = pl.BlockSpec(memory_space=pl.ANY)
    dma = pltpu.SemaphoreType.DMA
    import_row = lambda a: a.reshape(1, -1)
    half = 2 * HEADS * HD
    return pl.pallas_call(
        lambda *refs: kernel(dp_x, *refs),
        out_shape=(
            jax.ShapeDtypeStruct(query.shape, BF16),
            jax.ShapeDtypeStruct(key.shape, BF16),
            jax.ShapeDtypeStruct(value.shape, BF16),
        ),
        in_specs=[vmem] * 4 + [smem] + [hbm] * 4,
        out_specs=[hbm] * 3,
        scratch_shapes=[
            pltpu.VMEM((2, 3 * CHIP, HEADS * HD), BF16),
            pltpu.VMEM((2, TOK, half), BF16),
            pltpu.VMEM((2, TOK, half), BF16),
            pltpu.VMEM((2, 5 * TOK, TOK), F32),
            pltpu.VMEM((2, CHIP, HD), F32),
            pltpu.VMEM((dp_z, dp_x, 8, 128), F32),
            pltpu.VMEM((HEADS, 2, CHIP, HD), F32),
            pltpu.VMEM((HEADS, 2, TOK, HD), F32),
            pltpu.VMEM((HEADS, 2, CHIP, HD), BF16),
            pltpu.VMEM((HEADS, 2, CHIP, HD), BF16),
            pltpu.VMEM((HEADS, 2, CHIP, HD), BF16),
            pltpu.VMEM((HEADS, 2, 2, TOK, HD), BF16),
            pltpu.VMEM((HEADS, 2, TOK, HD), BF16),
            pltpu.VMEM((HEADS, 2, TOK, HD), BF16),
            pltpu.VMEM((TOK, half), BF16),
            pltpu.VMEM((TOK, half), BF16),
            pltpu.VMEM((2, TOK, half), BF16),
            dma((HEADS, 2, 2)),
            dma((HEADS, 2, 2)),
            dma((HEADS, 2)),
            dma((HEADS, 2)),
            dma((HEADS, 2)),
            dma((HEADS, 2)),
            dma((HEADS, 2, 2)),
            dma((HEADS, 2, 2)),
            dma((HEADS, 2)),
            dma((HEADS, 2)),
            dma((4,)),
            dma((4,)),
            dma((HEADS,)),
            dma((HEADS,)),
            dma((4,)),
            dma((HEADS,)),
            dma((HEADS, 2, 2)),
            dma((dp_x - 1,)),
            dma((dp_x - 1,)),
            dma((dp_z - 1,)),
            dma((dp_z - 1,)),
        ],
        compiler_params=pltpu.CompilerParams(
            collective_id=0, has_side_effects=True, vmem_limit_bytes=48 * 1024 * 1024
        ),
        cost_estimate=pl.CostEstimate(flops=2_000_000_000, bytes_accessed=4_000_000, transcendentals=4_000_000),
    )(
        import_row(reward),
        import_row(group_id),
        import_row(keep),
        import_row(dest),
        doc_len,
        query,
        key,
        value,
        grad_out,
    )


def solution(mesh):
    return jax.shard_map(
        body,
        mesh=mesh,
        in_specs=(
            P("dp"),
            P("dp"),
            P("dp"),
            P("dp"),
            P("dp", None),
            P(("dp", "tensor"), None),
            P(("dp", "tensor"), None),
            P(("dp", "tensor"), None),
            P(("dp", "tensor"), None),
        ),
        out_specs=(P(("dp", "tensor"), None), P(("dp", "tensor"), None), P(("dp", "tensor"), None)),
        check_vma=False,
    )
```

```python
import math

import jax
import jax.numpy as jnp
from jax import lax
from jax.experimental import pallas as pl
from jax.experimental.pallas import tpu as pltpu
from jax.sharding import PartitionSpec as P

HD = 128
TOK = 128
CHIP = 2 * TOK
SLOTS = 8
GROUP = 16
ROLL = 12
PIECES = 2
HEADS = 4
MESH = pl.DeviceIdType.MESH
F32 = jnp.float32
BF16 = jnp.bfloat16

softcap = 50.0
to_capped = 1.0 / (12.0 * softcap)
to_exponent = softcap * math.log2(math.e)


def head_cols(index, width=1):
    return pl.ds(pl.multiple_of(index * HD, HD), width * HD)


def rows_of(start):
    return pl.ds(pl.multiple_of(start, TOK), TOK)


def advantage_table(all_ref, groups, row):
    planes = all_ref.shape[0] * all_ref.shape[1]

    def field(n):
        return jnp.concatenate(
            [all_ref[i // all_ref.shape[1], i % all_ref.shape[1], n : n + 1, :] for i in range(planes)], axis=0
        )

    reward, group, keep, dest = field(0), field(1), field(2), field(3)
    counts, sums, squares = [], [], []
    for g in range(groups):
        member = jnp.where(group == float(g), keep, 0.0)
        counts.append(jnp.sum(member, axis=0, keepdims=True))
        sums.append(jnp.sum(member * reward, axis=0, keepdims=True))
        squares.append(jnp.sum(member * reward * reward, axis=0, keepdims=True))

    def total(parts):
        return jnp.sum(jnp.concatenate(parts, axis=0), axis=1, keepdims=True)

    members = jnp.maximum(total(counts), 1.0)
    average = total(sums) / members
    spread = jnp.sqrt(jnp.maximum(total(squares) / members - average * average, 0.0))
    divisor = jnp.maximum(spread, 1.0)
    row_mean = jnp.zeros_like(reward)
    row_divisor = jnp.zeros_like(reward)
    for g in range(groups):
        own = group == float(g)
        row_mean = jnp.where(own, average[g : g + 1, :], row_mean)
        row_divisor = jnp.where(own, divisor[g : g + 1, :], row_divisor)
    row_divisor = jnp.maximum(row_divisor, 1.0)
    advantage = keep * (reward - row_mean) / row_divisor
    slots = []
    for s in range(SLOTS):
        wanted = (row * SLOTS + s).astype(F32)
        slots.append(jnp.sum(jnp.where(dest == wanted, advantage, 0.0), axis=0, keepdims=True))
    return total(slots)


def kernel(
    dp_x,
    reward_hbm,
    group_hbm,
    keep_hbm,
    dest_hbm,
    doc_ref,
    q_hbm,
    k_hbm,
    v_hbm,
    g_hbm,
    dq_hbm,
    dk_hbm,
    dv_hbm,
    kv,
    qs,
    gs,
    mask,
    weight,
    reward_ref,
    group_ref,
    keep_ref,
    dest_ref,
    rolls,
    table_ref,
    near,
    mine,
    far_out,
    far_in,
    near_out,
    near_in,
    side_out,
    side_in,
    dq_raw,
    dq_own,
    dq_side,
    done,
    own_ss,
    own_rs,
    relay_ss,
    relay_rs,
    far_ss,
    far_rs,
    near_ss,
    near_rs,
    side_ss,
    side_rs,
    pair_ss,
    pair_rs,
    dq_ss,
    dq_rs,
    load_s,
    small_s,
    store_s,
    out_s,
    x_ss,
    x_rs,
    z_ss,
    z_rs,
    table_ss,
    table_rs,
):
    dp = lax.axis_index("dp")
    ti = lax.axis_index("tensor")
    chips = lax.axis_size("tensor") // 2
    dp_z = lax.axis_size("dp") // dp_x
    chip, core = ti // 2, ti % 2
    other = 1 - core
    last = chips - 1
    px, pz = dp % dp_x, dp // dp_x

    def at(c, k):
        return (dp, 2 * c + k)

    sibling = at(chip, other)
    x_peers = [(pz * dp_x + (px + i) % dp_x, ti) for i in range(1, dp_x)]
    z_peers = [(((pz + i) % dp_z) * dp_x + px, ti) for i in range(1, dp_z)]

    def remote(src, dst, ss, rs, device):
        return pltpu.make_async_remote_copy(
            src_ref=src, dst_ref=dst, send_sem=ss, recv_sem=rs, device_id=device, device_id_type=MESH
        )

    barrier = pltpu.get_barrier_semaphore()

    def greet(devices):
        for device in devices:
            pl.semaphore_signal(barrier, inc=1, device_id=device, device_id_type=MESH)

    greet([sibling])

    @pl.when(chip < last)
    def _():
        greet([at(chip + 1, 0), at(chip + 1, 1)])

    @pl.when(chip > 0)
    def _():
        greet([at(chip - 1, 0), at(chip - 1, 1)])

    @pl.when(chip < last - 1)
    def _():
        greet([at(last, core)])

    @pl.when(chip == last)
    def _():
        greet(x_peers + z_peers)

    half = 2 * HEADS * HD
    own_half = pl.ds(pl.multiple_of(core * half, half), half)
    side_half = pl.ds(pl.multiple_of(other * half, half), half)
    own_kv = pl.ds(pl.multiple_of(core * (half // 2), half // 2), half // 2)
    side_kv = pl.ds(pl.multiple_of(other * (half // 2), half // 2), half // 2)
    own_rows = rows_of(2 * CHIP + core * TOK)
    side_rows = rows_of(2 * CHIP + other * TOK)
    loads = [
        pltpu.make_async_copy(k_hbm.at[:, own_kv], kv.at[0, own_rows], load_s.at[0]),
        pltpu.make_async_copy(v_hbm.at[:, own_kv], kv.at[1, own_rows], load_s.at[1]),
        pltpu.make_async_copy(q_hbm.at[:, own_half], qs.at[core], load_s.at[2]),
        pltpu.make_async_copy(g_hbm.at[:, own_half], gs.at[core], load_s.at[3]),
    ]
    small_loads = [
        pltpu.make_async_copy(reward_hbm, reward_ref, small_s.at[0]),
        pltpu.make_async_copy(group_hbm, group_ref, small_s.at[1]),
        pltpu.make_async_copy(keep_hbm, keep_ref, small_s.at[2]),
        pltpu.make_async_copy(dest_hbm, dest_ref, small_s.at[3]),
    ]

    def own_copy(h, i, k):
        src = (k_hbm, v_hbm)[i]
        return remote(
            src.at[:, head_cols(HEADS * k + h)],
            kv.at[i, rows_of(CHIP + core * TOK), head_cols(h)],
            own_ss.at[h, i, k],
            own_rs.at[h, i, core],
            at(chip + 1, k),
        )

    def own_arrival(h, i, k):
        dst = kv.at[i, rows_of(CHIP + k * TOK), head_cols(h)]
        return remote(dst, dst, own_ss.at[h, i, k], own_rs.at[h, i, k], at(chip - 1, k))

    def relay_copy(h, i):
        return remote(
            kv.at[i, pl.ds(CHIP, CHIP), head_cols(h)],
            kv.at[i, pl.ds(0, CHIP), head_cols(h)],
            relay_ss.at[h, i],
            relay_rs.at[h, i],
            at(chip + 1, core),
        )

    def far_copy(h, i):
        return remote(far_out.at[h, i], far_in.at[h, i], far_ss.at[h, i], far_rs.at[h, i], at(chip - 1, core))

    def near_copy(h, i, k):
        return remote(
            near_out.at[h, i, pl.ds(k * TOK, TOK)],
            near_in.at[h, i, core],
            near_ss.at[h, i, k],
            near_rs.at[h, i, core],
            at(chip - 1, k),
        )

    def near_arrival(h, i, k):
        dst = near_in.at[h, i, k]
        return remote(dst, dst, near_ss.at[h, i, k], near_rs.at[h, i, k], at(chip + 1, k))

    def side_copy(h, i):
        return remote(side_out.at[h, i], side_in.at[h, i], side_ss.at[h, i], side_rs.at[h, i], sibling)

    def dq_copy(h):
        return remote(
            dq_side.at[:, head_cols(2 * h, 2)],
            dq_hbm.at[:, head_cols(2 * HEADS * core + 2 * h, 2)],
            dq_ss.at[h],
            dq_rs.at[h],
            sibling,
        )

    def dq_arrival(h):
        dst = dq_hbm.at[:, head_cols(2 * HEADS * other + 2 * h, 2)]
        return remote(dst, dst, dq_ss.at[h], dq_rs.at[h], sibling)

    def dq_store(h):
        return pltpu.make_async_copy(
            dq_own.at[:, head_cols(2 * h, 2)],
            dq_hbm.at[:, head_cols(2 * HEADS * core + 2 * h, 2)],
            store_s.at[h],
        )

    def out_store(h, i, k):
        return pltpu.make_async_copy(
            done.at[i, :, head_cols(HEADS * k + h)],
            (dk_hbm, dv_hbm)[i].at[:, head_cols(HEADS * k + h)],
            out_s.at[h, i, k],
        )

    def pair_copy(n, rows, place):
        src = (k_hbm, v_hbm, q_hbm, g_hbm)[n].at[:, side_kv if n < 2 else side_half]
        dst = kv.at[n, rows] if n < 2 else (qs, gs)[n - 2].at[place]
        return remote(src, dst, pair_ss.at[n], pair_rs.at[n], sibling)

    def x_copy(i):
        return remote(rolls.at[pz, px], rolls.at[pz, px], x_ss.at[i - 1], x_rs.at[i - 1], x_peers[i - 1])

    def x_arrival(i):
        sender = (px + dp_x - i) % dp_x
        arrived = rolls.at[pz, sender]
        return remote(arrived, arrived, x_ss.at[i - 1], x_rs.at[i - 1], (pz * dp_x + sender, ti))

    def z_copy(i):
        return remote(rolls.at[pz], rolls.at[pz], z_ss.at[i - 1], z_rs.at[i - 1], z_peers[i - 1])

    def z_arrival(i):
        sender = (pz + dp_z - i) % dp_z
        arrived = rolls.at[sender]
        return remote(arrived, arrived, z_ss.at[i - 1], z_rs.at[i - 1], (sender * dp_x + px, ti))

    def table_copy(c):
        return remote(table_ref, table_ref, table_ss.at[c], table_rs, at(c, core))

    def start_own(h, k):
        for i in range(2):
            own_copy(h, i, k).start()

    def start_pair():
        for n in range(4):
            pair_copy(n, own_rows, core).start()

    @pl.when(chip == last)
    def _():
        for copy in small_loads:
            copy.start()

    @pl.when(chip < last)
    def _():
        pl.semaphore_wait(barrier, jnp.where(chip == 0, 3, 5))
        start_own(0, 0)
        start_own(0, 1)
        start_own(1, 0)
        start_pair()

    for copy in loads:
        copy.start()

    @pl.when(chip < 2)
    def _():
        kv[:, 0:CHIP] = jnp.zeros((2, CHIP, HEADS * HD), BF16)

    @pl.when(chip == 0)
    def _():
        kv[:, CHIP : 2 * CHIP] = jnp.zeros((2, CHIP, HEADS * HD), BF16)

    @pl.when((chip == 0) | (chip == last))
    def _():
        far_in[...] = jnp.zeros_like(far_in)

    ends = []
    for s in range(SLOTS):
        ends.append(doc_ref[0, s] + (ends[-1] if s else 0))
    for b in range(2):
        query_pos = chip * CHIP + b * TOK + lax.broadcasted_iota(jnp.int32, (1, TOK), 1)
        first = jnp.zeros_like(query_pos)
        for s in range(SLOTS - 1):
            first = jnp.where(query_pos >= ends[s], ends[s], first)
        key_pos = (chip - 2) * CHIP + b * TOK + lax.broadcasted_iota(jnp.int32, (5 * TOK, TOK), 0)
        mask[b] = jnp.where((key_pos <= query_pos) & (key_pos >= first), 1.0, 0.0)

    @pl.when(chip == last)
    def _():
        near_in[...] = jnp.zeros_like(near_in)
        sub = lax.broadcasted_iota(jnp.int32, (8, 128), 0)
        rolls[pz, px] = jnp.where((sub == 1) | (sub == 3), -1.0, 0.0)
        for copy in small_loads:
            copy.wait()
        rolls[pz, px, 0:1, 0:ROLL] = reward_ref[...]
        rolls[pz, px, 1:2, 0:ROLL] = group_ref[...].astype(F32)
        rolls[pz, px, 2:3, 0:ROLL] = keep_ref[...].astype(F32)
        rolls[pz, px, 3:4, 0:ROLL] = dest_ref[...].astype(F32)
        pl.semaphore_wait(barrier, 3 + (last - 1) + (dp_x - 1) + (dp_z - 1))
        start_pair()
        for i in range(1, dp_x):
            x_copy(i).start()
        for i in range(1, dp_x):
            x_arrival(i).wait_recv()
        for i in range(1, dp_z):
            z_copy(i).start()

    def await_own(h):
        @pl.when(chip > 0)
        def _():
            for i in range(2):
                for k in range(2):
                    own_arrival(h, i, k).wait_recv()

    def pass_on(h):
        await_own(h)

        @pl.when((chip > 0) & (chip < last))
        def _():
            for i in range(2):
                relay_copy(h, i).start()

        @pl.when((chip < last) & (h + 1 < HEADS))
        def _():
            start_own(h + 1, 1)

        @pl.when((chip < last) & (h + 2 < HEADS))
        def _():
            start_own(h + 2, 0)

    def stacked(ref, b, h):
        return jnp.concatenate([ref[b, :, head_cols(2 * h)], ref[b, :, head_cols(2 * h + 1)]], axis=0)

    def dot(a, b, dims):
        return lax.dot_general(a, b, (dims, ((), ())), preferred_element_type=F32)

    def terms(h, b):
        window = pl.ds(b * TOK, 5 * TOK)
        keys = kv[0, window, head_cols(h)]
        values = kv[1, window, head_cols(h)]
        query, grad = stacked(qs, b, h), stacked(gs, b, h)
        allowed = mask[b]
        capped = jnp.tanh(dot(keys, query, ((1,), (1,))) * to_capped)
        weights = jnp.exp2(capped * to_exponent) * jnp.concatenate([allowed, allowed], axis=1)
        prob_grad = dot(values, grad, ((1,), (1,)))
        inverse = 1.0 / jnp.sum(weights, axis=0, keepdims=True)
        delta = jnp.sum(weights * prob_grad, axis=0, keepdims=True) * inverse
        probs = weights * inverse
        logit_grad = (probs * (prob_grad - delta) * (1.0 - capped * capped)).astype(BF16)
        dv = dot(probs.astype(BF16), grad, ((1,), (0,)))
        dk = dot(logit_grad, query, ((1,), (0,)))
        dq = dot(logit_grad, keys, ((0,), (0,)))
        return dk, dv, dq

    def work(h):
        @pl.when(chip > 1)
        def _():
            for i in range(2):
                relay_copy(h, i).wait_recv()

        first, second = terms(h, 0), terms(h, 1)
        for i in range(2):
            a, b = first[i], second[i]
            far_out[h, i, 0:TOK] = a[0:TOK].astype(BF16)
            far_out[h, i, TOK:CHIP] = (a[TOK:CHIP] + b[0:TOK]).astype(BF16)

        @pl.when(chip > 1)
        def _():
            for i in range(2):
                far_copy(h, i).start()

        for i in range(2):
            a, b = first[i], second[i]
            near[h, i] = a[CHIP : 2 * CHIP] + b[TOK : TOK + CHIP]
            own_part = (a[4 * TOK : 5 * TOK] + b[3 * TOK : 4 * TOK], b[4 * TOK : 5 * TOK])
            mine[h, i] = jnp.where(core == 0, own_part[0], own_part[1])
            side_out[h, i] = jnp.where(core == 0, own_part[1], own_part[0]).astype(BF16)
            side_copy(h, i).start()
        for b, part in ((0, first[2]), (1, second[2])):
            for r in range(2):
                dq_raw[h, b, r] = part[r * TOK : (r + 1) * TOK]

    def pass_back(h):
        @pl.when(chip > 0)
        def _():
            for i in range(2):

                @pl.when(chip < last)
                def _():
                    far_copy(h, i).wait_recv()

                near_out[h, i] = (near[h, i] + far_in[h, i].astype(F32)).astype(BF16)
                for k in range(2):
                    near_copy(h, i, k).start()

    def emit_queries(h):
        for b, ref in ((core, dq_own), (other, dq_side)):
            scale = weight[1, rows_of(b * TOK)]
            for r in range(2):
                ref[:, head_cols(2 * h + r)] = (dq_raw[h, b, r] * scale).astype(BF16)
        dq_store(h).start()
        dq_copy(h).start()

    def finish(h):
        for i in range(2):
            scale = weight[1 - i, rows_of(core * TOK)]
            side_copy(h, i).wait_recv()

            @pl.when(chip < last)
            def _():
                for k in range(2):
                    near_arrival(h, i, k).wait_recv()

            a = mine[h, i] + near_in[h, i, core].astype(F32)
            b = side_in[h, i].astype(F32) + near_in[h, i, other].astype(F32)
            done[i, :, head_cols(HEADS * core + h)] = (a * scale).astype(BF16)
            done[i, :, head_cols(HEADS * other + h)] = (b * scale).astype(BF16)
            for k in range(2):
                out_store(h, i, k).start()

    def make_table():
        @pl.when(chip == last)
        def _():
            for i in range(1, dp_z):
                z_arrival(i).wait_recv()
            groups = lax.axis_size("dp") * ROLL // GROUP
            table_ref[...] = advantage_table(rolls, groups, dp) + jnp.zeros((SLOTS, 128), F32)
            for c in range(last):
                table_copy(c).start()

    def make_weight():
        @pl.when(chip < last)
        def _():
            remote(table_ref, table_ref, table_ss.at[0], table_rs, at(last, core)).wait_recv()

        token = chip * CHIP + lax.broadcasted_iota(jnp.int32, (CHIP, HD), 0)
        factor = jnp.zeros((CHIP, HD), F32) + table_ref[0:1, :]
        for s in range(1, SLOTS):
            factor = jnp.where(token >= ends[s - 1], table_ref[s : s + 1, :], factor)
        weight[0] = factor
        weight[1] = factor * (1.0 / 12.0)

    pass_on(0)
    pass_on(1)
    for copy in loads:
        copy.wait()
    for n in range(4):
        pair_copy(n, side_rows, other).wait_recv()

    def turn(h, carry):
        work(h)

        @pl.when(h == 0)
        def _():
            make_table()

        @pl.when(h > 0)
        def _():
            pass_back(h - 1)

        @pl.when((h > 0) & (h + 1 < HEADS))
        def _():
            pass_on(h + 1)

        @pl.when(h == 2)
        def _():
            make_weight()
            emit_queries(0)
            emit_queries(1)

        @pl.when(h > 1)
        def _():
            emit_queries(h)
            finish(h - 2)

        return carry

    lax.fori_loop(0, HEADS, turn, 0)
    pass_back(HEADS - 1)
    finish(HEADS - 2)
    finish(HEADS - 1)

    @pl.when(chip == last)
    def _():
        for i in range(1, dp_x):
            x_copy(i).wait_send()
        for i in range(1, dp_z):
            z_copy(i).wait_send()
        for c in range(last):
            table_copy(c).wait_send()

    for n in range(4):
        pair_copy(n, own_rows, core).wait_send()

    def settle(h, carry):
        for i in range(2):
            for k in range(2):
                out_store(h, i, k).wait()

            @pl.when(chip < last)
            def _():
                for k in range(2):
                    own_copy(h, i, k).wait_send()

            @pl.when(chip > 0)
            def _():
                for k in range(2):
                    near_copy(h, i, k).wait_send()

            @pl.when((chip > 0) & (chip < last))
            def _():
                relay_copy(h, i).wait_send()

            @pl.when(chip > 1)
            def _():
                far_copy(h, i).wait_send()

            side_copy(h, i).wait_send()
        dq_store(h).wait()
        dq_copy(h).wait_send()
        dq_arrival(h).wait_recv()
        return carry

    lax.fori_loop(0, HEADS, settle, 0)


def hand_over(*refs):
    sources, results, stages, in_sem, out_sem = refs[:3], refs[3:6], refs[6:9], refs[9], refs[10]
    loads, stores = [], []
    for n in range(3):
        for p in range(PIECES):
            rows = pl.ds(p * (TOK // PIECES), TOK // PIECES)
            loads.append(pltpu.make_async_copy(sources[n].at[rows], stages[n].at[rows], in_sem.at[n, p]))
            stores.append(pltpu.make_async_copy(stages[n].at[rows], results[n].at[rows], out_sem.at[n, p]))
    for copy in loads:
        copy.start()
    for load, store in zip(loads, stores):
        load.wait()
        store.start()
    for copy in stores:
        copy.wait()


def body(reward, group_id, keep, dest, doc_len, query, key, value, grad_out):
    dp_size = lax.axis_size("dp")
    dp_x = 4 if dp_size % 32 == 0 else 2
    dp_z = dp_size // dp_x
    smem = pl.BlockSpec(memory_space=pltpu.SMEM)
    hbm = pl.BlockSpec(memory_space=pl.ANY)
    dma = pltpu.SemaphoreType.DMA
    import_row = lambda a: a.reshape(1, -1)
    half = 2 * HEADS * HD
    shapes = tuple(jax.ShapeDtypeStruct(a.shape, BF16) for a in (query, key, value))
    results = pl.pallas_call(
        lambda *refs: kernel(dp_x, *refs),
        out_shape=shapes,
        in_specs=[hbm] * 4 + [smem] + [hbm] * 4,
        out_specs=[hbm] * 3,
        scratch_shapes=[
            pltpu.VMEM((2, 3 * CHIP, HEADS * HD), BF16),
            pltpu.VMEM((2, TOK, half), BF16),
            pltpu.VMEM((2, TOK, half), BF16),
            pltpu.VMEM((2, 5 * TOK, TOK), F32),
            pltpu.VMEM((2, CHIP, HD), F32),
            pltpu.VMEM((1, ROLL), F32),
            pltpu.VMEM((1, ROLL), jnp.int32),
            pltpu.VMEM((1, ROLL), jnp.int32),
            pltpu.VMEM((1, ROLL), jnp.int32),
            pltpu.VMEM((dp_z, dp_x, 8, 128), F32),
            pltpu.VMEM((SLOTS, 128), F32),
            pltpu.VMEM((HEADS, 2, CHIP, HD), F32),
            pltpu.VMEM((HEADS, 2, TOK, HD), F32),
            pltpu.VMEM((HEADS, 2, CHIP, HD), BF16),
            pltpu.VMEM((HEADS, 2, CHIP, HD), BF16),
            pltpu.VMEM((HEADS, 2, CHIP, HD), BF16),
            pltpu.VMEM((HEADS, 2, 2, TOK, HD), BF16),
            pltpu.VMEM((HEADS, 2, TOK, HD), BF16),
            pltpu.VMEM((HEADS, 2, TOK, HD), BF16),
            pltpu.VMEM((HEADS, 2, 2, TOK, HD), F32),
            pltpu.VMEM((TOK, half), BF16),
            pltpu.VMEM((TOK, half), BF16),
            pltpu.VMEM((2, TOK, half), BF16),
            dma((HEADS, 2, 2)),
            dma((HEADS, 2, 2)),
            dma((HEADS, 2)),
            dma((HEADS, 2)),
            dma((HEADS, 2)),
            dma((HEADS, 2)),
            dma((HEADS, 2, 2)),
            dma((HEADS, 2, 2)),
            dma((HEADS, 2)),
            dma((HEADS, 2)),
            dma((4,)),
            dma((4,)),
            dma((HEADS,)),
            dma((HEADS,)),
            dma((4,)),
            dma((4,)),
            dma((HEADS,)),
            dma((HEADS, 2, 2)),
            dma((dp_x - 1,)),
            dma((dp_x - 1,)),
            dma((dp_z - 1,)),
            dma((dp_z - 1,)),
            dma((lax.axis_size("tensor") // 2 - 1,)),
            dma,
        ],
        compiler_params=pltpu.CompilerParams(
            collective_id=0, has_side_effects=True, vmem_limit_bytes=60 * 1024 * 1024
        ),
        cost_estimate=pl.CostEstimate(flops=2_000_000_000, bytes_accessed=4_000_000, transcendentals=4_000_000),
    )(
        import_row(reward),
        import_row(group_id),
        import_row(keep),
        import_row(dest),
        doc_len,
        query,
        key,
        value,
        grad_out,
    )
    return pl.pallas_call(
        hand_over,
        out_shape=shapes,
        in_specs=[hbm] * 3,
        out_specs=[hbm] * 3,
        scratch_shapes=[pltpu.VMEM(a.shape, BF16) for a in shapes] + [dma((3, PIECES)), dma((3, PIECES))],
        compiler_params=pltpu.CompilerParams(vmem_limit_bytes=60 * 1024 * 1024),
    )(*results)


def solution(mesh):
    return jax.shard_map(
        body,
        mesh=mesh,
        in_specs=(
            P("dp"),
            P("dp"),
            P("dp"),
            P("dp"),
            P("dp", None),
            P(("dp", "tensor"), None),
            P(("dp", "tensor"), None),
            P(("dp", "tensor"), None),
            P(("dp", "tensor"), None),
        ),
        out_specs=(P(("dp", "tensor"), None), P(("dp", "tensor"), None), P(("dp", "tensor"), None)),
        check_vma=False,
    )
```

```python
import math

import jax
import jax.numpy as jnp
from jax import lax
from jax.experimental import pallas as pl
from jax.experimental.pallas import tpu as pltpu
from jax.sharding import PartitionSpec as P

HD = 128
TOK = 128
CHIP = 2 * TOK
SLOTS = 8
GROUP = 16
ROLL = 12
PIECES = 2
AHEAD = 3
HEADS = 4
MESH = pl.DeviceIdType.MESH
F32 = jnp.float32
BF16 = jnp.bfloat16

softcap = 50.0
to_capped = 1.0 / (12.0 * softcap)
to_exponent = softcap * math.log2(math.e)


def head_cols(index, width=1):
    return pl.ds(pl.multiple_of(index * HD, HD), width * HD)


def rows_of(start):
    return pl.ds(pl.multiple_of(start, TOK), TOK)


def advantage_table(all_ref, groups, row):
    planes = all_ref.shape[0] * all_ref.shape[1]

    def field(n):
        return jnp.concatenate(
            [all_ref[i // all_ref.shape[1], i % all_ref.shape[1], n : n + 1, :] for i in range(planes)], axis=0
        )

    reward, group, keep, dest = field(0), field(1), field(2), field(3)
    counts, sums, squares = [], [], []
    for g in range(groups):
        member = jnp.where(group == float(g), keep, 0.0)
        counts.append(jnp.sum(member, axis=0, keepdims=True))
        sums.append(jnp.sum(member * reward, axis=0, keepdims=True))
        squares.append(jnp.sum(member * reward * reward, axis=0, keepdims=True))

    def total(parts):
        return jnp.sum(jnp.concatenate(parts, axis=0), axis=1, keepdims=True)

    members = jnp.maximum(total(counts), 1.0)
    average = total(sums) / members
    spread = jnp.sqrt(jnp.maximum(total(squares) / members - average * average, 0.0))
    divisor = jnp.maximum(spread, 1.0)
    row_mean = jnp.zeros_like(reward)
    row_divisor = jnp.zeros_like(reward)
    for g in range(groups):
        own = group == float(g)
        row_mean = jnp.where(own, average[g : g + 1, :], row_mean)
        row_divisor = jnp.where(own, divisor[g : g + 1, :], row_divisor)
    row_divisor = jnp.maximum(row_divisor, 1.0)
    advantage = keep * (reward - row_mean) / row_divisor
    slots = []
    for s in range(SLOTS):
        wanted = (row * SLOTS + s).astype(F32)
        slots.append(jnp.sum(jnp.where(dest == wanted, advantage, 0.0), axis=0, keepdims=True))
    return total(slots)


def kernel(
    dp_x,
    reward_hbm,
    group_hbm,
    keep_hbm,
    dest_hbm,
    doc_ref,
    q_hbm,
    k_hbm,
    v_hbm,
    g_hbm,
    dq_hbm,
    dk_hbm,
    dv_hbm,
    kv,
    qs,
    gs,
    mask,
    probs,
    slope,
    weight,
    reward_ref,
    group_ref,
    keep_ref,
    dest_ref,
    rolls,
    table_ref,
    near,
    mine,
    far_out,
    far_in,
    near_out,
    near_in,
    side_out,
    side_in,
    dq_raw,
    dq_own,
    dq_side,
    done,
    own_ss,
    own_rs,
    relay_ss,
    relay_rs,
    far_ss,
    far_rs,
    near_ss,
    near_rs,
    side_ss,
    side_rs,
    pair_ss,
    pair_rs,
    dq_ss,
    dq_rs,
    load_s,
    small_s,
    store_s,
    out_s,
    x_ss,
    x_rs,
    z_ss,
    z_rs,
    table_ss,
    table_rs,
):
    dp = lax.axis_index("dp")
    ti = lax.axis_index("tensor")
    chips = lax.axis_size("tensor") // 2
    dp_z = lax.axis_size("dp") // dp_x
    chip, core = ti // 2, ti % 2
    other = 1 - core
    last = chips - 1
    px, pz = dp % dp_x, dp // dp_x

    def at(c, k):
        return (dp, 2 * c + k)

    sibling = at(chip, other)
    x_peers = [(pz * dp_x + (px + i) % dp_x, ti) for i in range(1, dp_x)]
    z_peers = [(((pz + i) % dp_z) * dp_x + px, ti) for i in range(1, dp_z)]

    def remote(src, dst, ss, rs, device):
        return pltpu.make_async_remote_copy(
            src_ref=src, dst_ref=dst, send_sem=ss, recv_sem=rs, device_id=device, device_id_type=MESH
        )

    barrier = pltpu.get_barrier_semaphore()

    def greet(devices):
        for device in devices:
            pl.semaphore_signal(barrier, inc=1, device_id=device, device_id_type=MESH)

    greet([sibling])

    @pl.when(chip > 0)
    def _():
        greet([at(chip - 1, 0), at(chip - 1, 1)])

    @pl.when(chip < last)
    def _():
        greet([at(last, core)])

    @pl.when(chip == last)
    def _():
        greet(x_peers + z_peers)

    half = 2 * HEADS * HD
    own_half = pl.ds(pl.multiple_of(core * half, half), half)
    side_half = pl.ds(pl.multiple_of(other * half, half), half)
    own_kv = pl.ds(pl.multiple_of(core * (half // 2), half // 2), half // 2)
    side_kv = pl.ds(pl.multiple_of(other * (half // 2), half // 2), half // 2)
    own_rows = rows_of(2 * CHIP + core * TOK)
    side_rows = rows_of(2 * CHIP + other * TOK)
    loads = [
        pltpu.make_async_copy(k_hbm.at[:, own_kv], kv.at[0, own_rows], load_s.at[0]),
        pltpu.make_async_copy(v_hbm.at[:, own_kv], kv.at[1, own_rows], load_s.at[1]),
        pltpu.make_async_copy(q_hbm.at[:, own_half], qs.at[core], load_s.at[2]),
        pltpu.make_async_copy(g_hbm.at[:, own_half], gs.at[core], load_s.at[3]),
    ]
    small_loads = [
        pltpu.make_async_copy(reward_hbm, reward_ref, small_s.at[0]),
        pltpu.make_async_copy(group_hbm, group_ref, small_s.at[1]),
        pltpu.make_async_copy(keep_hbm, keep_ref, small_s.at[2]),
        pltpu.make_async_copy(dest_hbm, dest_ref, small_s.at[3]),
    ]

    def own_copy(h, i, k):
        src = (k_hbm, v_hbm)[i]
        return remote(
            src.at[:, head_cols(HEADS * k + h)],
            kv.at[i, rows_of(CHIP + core * TOK), head_cols(h)],
            own_ss.at[h, i, k],
            own_rs.at[h, i, core],
            at(chip + 1, k),
        )

    def own_arrival(h, i, k):
        dst = kv.at[i, rows_of(CHIP + k * TOK), head_cols(h)]
        return remote(dst, dst, own_ss.at[h, i, k], own_rs.at[h, i, k], at(chip - 1, k))

    def relay_copy(h, i):
        return remote(
            kv.at[i, pl.ds(CHIP, CHIP), head_cols(h)],
            kv.at[i, pl.ds(0, CHIP), head_cols(h)],
            relay_ss.at[h, i],
            relay_rs.at[h, i],
            at(chip + 1, core),
        )

    def far_copy(h, i):
        return remote(far_out.at[h, i], far_in.at[h, i], far_ss.at[h, i], far_rs.at[h, i], at(chip - 1, core))

    def near_copy(h, i, k):
        return remote(
            near_out.at[h, i, pl.ds(k * TOK, TOK)],
            near_in.at[h, i, core],
            near_ss.at[h, i, k],
            near_rs.at[h, i, core],
            at(chip - 1, k),
        )

    def near_arrival(h, i, k):
        dst = near_in.at[h, i, k]
        return remote(dst, dst, near_ss.at[h, i, k], near_rs.at[h, i, k], at(chip + 1, k))

    def side_copy(h, i):
        return remote(side_out.at[h, i], side_in.at[h, i], side_ss.at[h, i], side_rs.at[h, i], sibling)

    def dq_copy(h):
        return remote(
            dq_side.at[:, head_cols(2 * h, 2)],
            dq_hbm.at[:, head_cols(2 * HEADS * core + 2 * h, 2)],
            dq_ss.at[h],
            dq_rs.at[h],
            sibling,
        )

    def dq_arrival(h):
        dst = dq_hbm.at[:, head_cols(2 * HEADS * other + 2 * h, 2)]
        return remote(dst, dst, dq_ss.at[h], dq_rs.at[h], sibling)

    def dq_store(h):
        return pltpu.make_async_copy(
            dq_own.at[:, head_cols(2 * h, 2)],
            dq_hbm.at[:, head_cols(2 * HEADS * core + 2 * h, 2)],
            store_s.at[h],
        )

    def out_store(h, i, k):
        return pltpu.make_async_copy(
            done.at[i, :, head_cols(HEADS * k + h)],
            (dk_hbm, dv_hbm)[i].at[:, head_cols(HEADS * k + h)],
            out_s.at[h, i, k],
        )

    def pair_copy(n, rows, place):
        src = (k_hbm, v_hbm, q_hbm, g_hbm)[n].at[:, side_kv if n < 2 else side_half]
        dst = kv.at[n, rows] if n < 2 else (qs, gs)[n - 2].at[place]
        return remote(src, dst, pair_ss.at[n], pair_rs.at[n], sibling)

    def x_copy(i):
        return remote(rolls.at[pz, px], rolls.at[pz, px], x_ss.at[i - 1], x_rs.at[i - 1], x_peers[i - 1])

    def x_arrival(i):
        sender = (px + dp_x - i) % dp_x
        arrived = rolls.at[pz, sender]
        return remote(arrived, arrived, x_ss.at[i - 1], x_rs.at[i - 1], (pz * dp_x + sender, ti))

    def z_copy(i):
        return remote(rolls.at[pz], rolls.at[pz], z_ss.at[i - 1], z_rs.at[i - 1], z_peers[i - 1])

    def z_arrival(i):
        sender = (pz + dp_z - i) % dp_z
        arrived = rolls.at[sender]
        return remote(arrived, arrived, z_ss.at[i - 1], z_rs.at[i - 1], (sender * dp_x + px, ti))

    def table_copy(c):
        return remote(table_ref, table_ref, table_ss.at[c], table_rs, at(c, core))

    def start_own(h, i):
        for k in range(2):
            own_copy(h, i, k).start()

    def start_pair():
        for n in range(4):
            pair_copy(n, own_rows, core).start()

    @pl.when(chip == last)
    def _():
        for copy in small_loads:
            copy.start()

    @pl.when(chip < last)
    def _():
        pl.semaphore_wait(barrier, 3)
        for n in range(AHEAD):
            start_own(n // 2, n % 2)
        start_pair()

    for copy in loads:
        copy.start()

    @pl.when(chip < 2)
    def _():
        kv[:, 0:CHIP] = jnp.zeros((2, CHIP, HEADS * HD), BF16)

    @pl.when(chip == 0)
    def _():
        kv[:, CHIP : 2 * CHIP] = jnp.zeros((2, CHIP, HEADS * HD), BF16)

    @pl.when((chip == 0) | (chip == last))
    def _():
        far_in[...] = jnp.zeros_like(far_in)

    ends = []
    for s in range(SLOTS):
        ends.append(doc_ref[0, s] + (ends[-1] if s else 0))
    for b in range(2):
        query_pos = chip * CHIP + b * TOK + lax.broadcasted_iota(jnp.int32, (1, TOK), 1)
        first = jnp.zeros_like(query_pos)
        for s in range(SLOTS - 1):
            first = jnp.where(query_pos >= ends[s], ends[s], first)
        key_pos = (chip - 2) * CHIP + b * TOK + lax.broadcasted_iota(jnp.int32, (5 * TOK, TOK), 0)
        mask[b] = jnp.where((key_pos <= query_pos) & (key_pos >= first), 1.0, 0.0)

    @pl.when(chip == last)
    def _():
        near_in[...] = jnp.zeros_like(near_in)
        sub = lax.broadcasted_iota(jnp.int32, (8, 128), 0)
        rolls[pz, px] = jnp.where((sub == 1) | (sub == 3), -1.0, 0.0)
        for copy in small_loads:
            copy.wait()
        rolls[pz, px, 0:1, 0:ROLL] = reward_ref[...]
        rolls[pz, px, 1:2, 0:ROLL] = group_ref[...].astype(F32)
        rolls[pz, px, 2:3, 0:ROLL] = keep_ref[...].astype(F32)
        rolls[pz, px, 3:4, 0:ROLL] = dest_ref[...].astype(F32)
        pl.semaphore_wait(barrier, 1 + last + (dp_x - 1) + (dp_z - 1))
        start_pair()
        for i in range(1, dp_x):
            x_copy(i).start()
        for i in range(1, dp_x):
            x_arrival(i).wait_recv()
        for i in range(1, dp_z):
            z_copy(i).start()

    def pass_on(h, i):
        @pl.when(chip > 0)
        def _():
            for k in range(2):
                own_arrival(h, i, k).wait_recv()

        @pl.when((chip > 0) & (chip < last))
        def _():
            relay_copy(h, i).start()

        later, kind = h + (i + AHEAD) // 2, (i + AHEAD) % 2

        @pl.when((chip < last) & (later < HEADS))
        def _():
            start_own(later, kind)

    def stacked(ref, b, h):
        return jnp.concatenate([ref[b, :, head_cols(2 * h)], ref[b, :, head_cols(2 * h + 1)]], axis=0)

    def dot(a, b, dims):
        return lax.dot_general(a, b, (dims, ((), ())), preferred_element_type=F32)

    def share_out(h, i, first, second):
        far_out[h, i, 0:TOK] = first[0:TOK].astype(BF16)
        far_out[h, i, TOK:CHIP] = (first[TOK:CHIP] + second[0:TOK]).astype(BF16)

        @pl.when(chip > 1)
        def _():
            far_copy(h, i).start()

        near[h, i] = first[CHIP : 2 * CHIP] + second[TOK : TOK + CHIP]
        own_part = (first[4 * TOK : 5 * TOK] + second[3 * TOK : 4 * TOK], second[4 * TOK : 5 * TOK])
        mine[h, i] = jnp.where(core == 0, own_part[0], own_part[1])
        side_out[h, i] = jnp.where(core == 0, own_part[1], own_part[0]).astype(BF16)
        side_copy(h, i).start()

    def await_relay(h, i):
        @pl.when(chip > 1)
        def _():
            relay_copy(h, i).wait_recv()

    def with_keys(h):
        await_relay(h, 0)
        value_grads = []
        for b in range(2):
            keys = kv[0, pl.ds(b * TOK, 5 * TOK), head_cols(h)]
            allowed = mask[b]
            capped = jnp.tanh(dot(keys, stacked(qs, b, h), ((1,), (1,))) * to_capped)
            weights = jnp.exp2(capped * to_exponent) * jnp.concatenate([allowed, allowed], axis=1)
            normal = weights * (1.0 / jnp.sum(weights, axis=0, keepdims=True))
            probs[b] = normal
            slope[b] = normal * (1.0 - capped * capped)
            value_grads.append(dot(normal.astype(BF16), stacked(gs, b, h), ((1,), (0,))))
        share_out(h, 1, *value_grads)

    def with_values(h):
        await_relay(h, 1)
        key_grads = []
        for b in range(2):
            window = pl.ds(b * TOK, 5 * TOK)
            prob_grad = dot(kv[1, window, head_cols(h)], stacked(gs, b, h), ((1,), (1,)))
            delta = jnp.sum(probs[b] * prob_grad, axis=0, keepdims=True)
            logit_grad = (slope[b] * (prob_grad - delta)).astype(BF16)
            key_grads.append(dot(logit_grad, stacked(qs, b, h), ((1,), (0,))))
            query_grad = dot(logit_grad, kv[0, window, head_cols(h)], ((0,), (0,)))
            for r in range(2):
                dq_raw[h, b, r] = query_grad[r * TOK : (r + 1) * TOK]
        share_out(h, 0, *key_grads)

    def pass_back(h, i):
        @pl.when(chip > 0)
        def _():
            @pl.when(chip < last)
            def _():
                far_copy(h, i).wait_recv()

            near_out[h, i] = (near[h, i] + far_in[h, i].astype(F32)).astype(BF16)
            for k in range(2):
                near_copy(h, i, k).start()

    def emit_queries(h):
        for b, ref in ((core, dq_own), (other, dq_side)):
            scale = weight[1, rows_of(b * TOK)]
            for r in range(2):
                ref[:, head_cols(2 * h + r)] = (dq_raw[h, b, r] * scale).astype(BF16)
        dq_store(h).start()
        dq_copy(h).start()

    def finish(h, i):
        scale = weight[1 - i, rows_of(core * TOK)]
        side_copy(h, i).wait_recv()

        @pl.when(chip < last)
        def _():
            for k in range(2):
                near_arrival(h, i, k).wait_recv()

        a = mine[h, i] + near_in[h, i, core].astype(F32)
        b = side_in[h, i].astype(F32) + near_in[h, i, other].astype(F32)
        done[i, :, head_cols(HEADS * core + h)] = (a * scale).astype(BF16)
        done[i, :, head_cols(HEADS * other + h)] = (b * scale).astype(BF16)
        for k in range(2):
            out_store(h, i, k).start()

    def make_table():
        @pl.when(chip == last)
        def _():
            for i in range(1, dp_z):
                z_arrival(i).wait_recv()
            groups = lax.axis_size("dp") * ROLL // GROUP
            table_ref[...] = advantage_table(rolls, groups, dp) + jnp.zeros((SLOTS, 128), F32)
            for c in range(last):
                table_copy(c).start()

    def make_weight():
        @pl.when(chip < last)
        def _():
            remote(table_ref, table_ref, table_ss.at[0], table_rs, at(last, core)).wait_recv()

        token = chip * CHIP + lax.broadcasted_iota(jnp.int32, (CHIP, HD), 0)
        factor = jnp.zeros((CHIP, HD), F32) + table_ref[0:1, :]
        for s in range(1, SLOTS):
            factor = jnp.where(token >= ends[s - 1], table_ref[s : s + 1, :], factor)
        weight[0] = factor
        weight[1] = factor * (1.0 / 12.0)

    pass_on(0, 0)
    pass_on(0, 1)
    for copy in loads:
        copy.wait()
    for n in range(4):
        pair_copy(n, side_rows, other).wait_recv()

    def turn(h, carry):
        @pl.when(h + 1 < HEADS)
        def _():
            pass_on(h + 1, 0)

        with_keys(h)

        @pl.when(h > 0)
        def _():
            pass_back(h - 1, 0)

        @pl.when(h == 1)
        def _():
            make_table()

        @pl.when(h + 1 < HEADS)
        def _():
            pass_on(h + 1, 1)

        with_values(h)
        pass_back(h, 1)
        return carry

    lax.fori_loop(0, HEADS, turn, 0)
    make_weight()
    for h in range(HEADS):
        emit_queries(h)
    pass_back(HEADS - 1, 0)
    for h in range(HEADS):
        finish(h, 1)
        finish(h, 0)

    @pl.when(chip == last)
    def _():
        for i in range(1, dp_x):
            x_copy(i).wait_send()
        for i in range(1, dp_z):
            z_copy(i).wait_send()
        for c in range(last):
            table_copy(c).wait_send()

    for n in range(4):
        pair_copy(n, own_rows, core).wait_send()

    def settle(h, carry):
        for i in range(2):
            for k in range(2):
                out_store(h, i, k).wait()

            @pl.when(chip < last)
            def _():
                for k in range(2):
                    own_copy(h, i, k).wait_send()

            @pl.when(chip > 0)
            def _():
                for k in range(2):
                    near_copy(h, i, k).wait_send()

            @pl.when((chip > 0) & (chip < last))
            def _():
                relay_copy(h, i).wait_send()

            @pl.when(chip > 1)
            def _():
                far_copy(h, i).wait_send()

            side_copy(h, i).wait_send()
        dq_store(h).wait()
        dq_copy(h).wait_send()
        dq_arrival(h).wait_recv()
        return carry

    lax.fori_loop(0, HEADS, settle, 0)


def hand_over(*refs):
    sources, results, stages, in_sem, out_sem = refs[:3], refs[3:6], refs[6:9], refs[9], refs[10]
    loads, stores = [], []
    for n in range(3):
        for p in range(PIECES):
            rows = pl.ds(p * (TOK // PIECES), TOK // PIECES)
            loads.append(pltpu.make_async_copy(sources[n].at[rows], stages[n].at[rows], in_sem.at[n, p]))
            stores.append(pltpu.make_async_copy(stages[n].at[rows], results[n].at[rows], out_sem.at[n, p]))
    for copy in loads:
        copy.start()
    for load, store in zip(loads, stores):
        load.wait()
        store.start()
    for copy in stores:
        copy.wait()


def body(reward, group_id, keep, dest, doc_len, query, key, value, grad_out):
    dp_size = lax.axis_size("dp")
    dp_x = 4 if dp_size % 32 == 0 else 2
    dp_z = dp_size // dp_x
    smem = pl.BlockSpec(memory_space=pltpu.SMEM)
    hbm = pl.BlockSpec(memory_space=pl.ANY)
    dma = pltpu.SemaphoreType.DMA
    import_row = lambda a: a.reshape(1, -1)
    half = 2 * HEADS * HD
    shapes = tuple(jax.ShapeDtypeStruct(a.shape, BF16) for a in (query, key, value))
    results = pl.pallas_call(
        lambda *refs: kernel(dp_x, *refs),
        out_shape=shapes,
        in_specs=[hbm] * 4 + [smem] + [hbm] * 4,
        out_specs=[hbm] * 3,
        scratch_shapes=[
            pltpu.VMEM((2, 3 * CHIP, HEADS * HD), BF16),
            pltpu.VMEM((2, TOK, half), BF16),
            pltpu.VMEM((2, TOK, half), BF16),
            pltpu.VMEM((2, 5 * TOK, TOK), F32),
            pltpu.VMEM((2, 5 * TOK, 2 * TOK), F32),
            pltpu.VMEM((2, 5 * TOK, 2 * TOK), F32),
            pltpu.VMEM((2, CHIP, HD), F32),
            pltpu.VMEM((1, ROLL), F32),
            pltpu.VMEM((1, ROLL), jnp.int32),
            pltpu.VMEM((1, ROLL), jnp.int32),
            pltpu.VMEM((1, ROLL), jnp.int32),
            pltpu.VMEM((dp_z, dp_x, 8, 128), F32),
            pltpu.VMEM((SLOTS, 128), F32),
            pltpu.VMEM((HEADS, 2, CHIP, HD), F32),
            pltpu.VMEM((HEADS, 2, TOK, HD), F32),
            pltpu.VMEM((HEADS, 2, CHIP, HD), BF16),
            pltpu.VMEM((HEADS, 2, CHIP, HD), BF16),
            pltpu.VMEM((HEADS, 2, CHIP, HD), BF16),
            pltpu.VMEM((HEADS, 2, 2, TOK, HD), BF16),
            pltpu.VMEM((HEADS, 2, TOK, HD), BF16),
            pltpu.VMEM((HEADS, 2, TOK, HD), BF16),
            pltpu.VMEM((HEADS, 2, 2, TOK, HD), F32),
            pltpu.VMEM((TOK, half), BF16),
            pltpu.VMEM((TOK, half), BF16),
            pltpu.VMEM((2, TOK, half), BF16),
            dma((HEADS, 2, 2)),
            dma((HEADS, 2, 2)),
            dma((HEADS, 2)),
            dma((HEADS, 2)),
            dma((HEADS, 2)),
            dma((HEADS, 2)),
            dma((HEADS, 2, 2)),
            dma((HEADS, 2, 2)),
            dma((HEADS, 2)),
            dma((HEADS, 2)),
            dma((4,)),
            dma((4,)),
            dma((HEADS,)),
            dma((HEADS,)),
            dma((4,)),
            dma((4,)),
            dma((HEADS,)),
            dma((HEADS, 2, 2)),
            dma((dp_x - 1,)),
            dma((dp_x - 1,)),
            dma((dp_z - 1,)),
            dma((dp_z - 1,)),
            dma((lax.axis_size("tensor") // 2 - 1,)),
            dma,
        ],
        compiler_params=pltpu.CompilerParams(
            collective_id=0, has_side_effects=True, vmem_limit_bytes=60 * 1024 * 1024
        ),
        cost_estimate=pl.CostEstimate(flops=2_000_000_000, bytes_accessed=4_000_000, transcendentals=4_000_000),
    )(
        import_row(reward),
        import_row(group_id),
        import_row(keep),
        import_row(dest),
        doc_len,
        query,
        key,
        value,
        grad_out,
    )
    return pl.pallas_call(
        hand_over,
        out_shape=shapes,
        in_specs=[hbm] * 3,
        out_specs=[hbm] * 3,
        scratch_shapes=[pltpu.VMEM(a.shape, BF16) for a in shapes] + [dma((3, PIECES)), dma((3, PIECES))],
        compiler_params=pltpu.CompilerParams(vmem_limit_bytes=60 * 1024 * 1024),
    )(*results)


def solution(mesh):
    return jax.shard_map(
        body,
        mesh=mesh,
        in_specs=(
            P("dp"),
            P("dp"),
            P("dp"),
            P("dp"),
            P("dp", None),
            P(("dp", "tensor"), None),
            P(("dp", "tensor"), None),
            P(("dp", "tensor"), None),
            P(("dp", "tensor"), None),
        ),
        out_specs=(P(("dp", "tensor"), None), P(("dp", "tensor"), None), P(("dp", "tensor"), None)),
        check_vma=False,
    )
```

```python
import math

import jax
import jax.numpy as jnp
from jax import lax
from jax.experimental import pallas as pl
from jax.experimental.pallas import tpu as pltpu
from jax.sharding import PartitionSpec as P

HD = 128
TOK = 128
CHIP = 2 * TOK
SLOTS = 8
GROUP = 16
ROLL = 12
AHEAD = 3
MID = 2
PLACES = ((0, 2, 3, 0), (3, 2, 4, 1), (7, 2, 2, 0), (9, 3, 1, 1))
HEADS = 4
MESH = pl.DeviceIdType.MESH
F32 = jnp.float32
BF16 = jnp.bfloat16

softcap = 50.0
to_capped = 1.0 / (12.0 * softcap)
to_exponent = softcap * math.log2(math.e)


def head_cols(index, width=1):
    return pl.ds(pl.multiple_of(index * HD, HD), width * HD)


def rows_of(start):
    return pl.ds(pl.multiple_of(start, TOK), TOK)


def advantage_table(all_ref, groups, row):
    def field(n):
        return jnp.concatenate([all_ref[i, n : n + 1, :] for i in range(all_ref.shape[0])], axis=0)

    reward, group, keep, dest = field(0), field(1), field(2), field(3)
    counts, sums, squares = [], [], []
    for g in range(groups):
        member = jnp.where(group == float(g), keep, 0.0)
        counts.append(jnp.sum(member, axis=0, keepdims=True))
        sums.append(jnp.sum(member * reward, axis=0, keepdims=True))
        squares.append(jnp.sum(member * reward * reward, axis=0, keepdims=True))

    def total(parts):
        return jnp.sum(jnp.concatenate(parts, axis=0), axis=1, keepdims=True)

    members = jnp.maximum(total(counts), 1.0)
    average = total(sums) / members
    spread = jnp.sqrt(jnp.maximum(total(squares) / members - average * average, 0.0))
    divisor = jnp.maximum(spread, 1.0)
    row_mean = jnp.zeros_like(reward)
    row_divisor = jnp.zeros_like(reward)
    for g in range(groups):
        own = group == float(g)
        row_mean = jnp.where(own, average[g : g + 1, :], row_mean)
        row_divisor = jnp.where(own, divisor[g : g + 1, :], row_divisor)
    row_divisor = jnp.maximum(row_divisor, 1.0)
    advantage = keep * (reward - row_mean) / row_divisor
    slots = []
    for s in range(SLOTS):
        wanted = (row * SLOTS + s).astype(F32)
        slots.append(jnp.sum(jnp.where(dest == wanted, advantage, 0.0), axis=0, keepdims=True))
    return total(slots)


def kernel(
    reward_hbm,
    group_hbm,
    keep_hbm,
    dest_hbm,
    doc_ref,
    q_hbm,
    k_hbm,
    v_hbm,
    g_hbm,
    dq_ref,
    dk_ref,
    dv_ref,
    kv,
    qs,
    gs,
    mask,
    probs,
    slope,
    weight,
    reward_ref,
    group_ref,
    keep_ref,
    dest_ref,
    rolls,
    table_ref,
    mask_next,
    q_next,
    mid_weights,
    mid_slope,
    mid_grads,
    stat_own,
    stat_next,
    stat_own_in,
    stat_next_in,
    dq_next,
    dq_next_in,
    near,
    mine,
    far_out,
    far_in,
    near_out,
    near_in,
    side_out,
    side_in,
    dq_raw,
    dq_side,
    own_ss,
    own_rs,
    relay_ss,
    relay_rs,
    far_ss,
    far_rs,
    near_ss,
    near_rs,
    side_ss,
    side_rs,
    pair_ss,
    pair_rs,
    dq_ss,
    dq_rs,
    load_s,
    small_s,
    roll_ss,
    roll_rs,
    table_ss,
    table_rs,
    next_ss,
    next_rs,
    stat_ss,
    stat_rs,
    dq_next_ss,
    dq_next_rs,
):
    dp = lax.axis_index("dp")
    ti = lax.axis_index("tensor")
    chips = lax.axis_size("tensor") // 2
    dp_size = lax.axis_size("dp")
    chip, core = ti // 2, ti % 2
    other = 1 - core
    last = chips - 1

    def at(c, k):
        return (dp, 2 * c + k)

    sibling = at(chip, other)
    def remote(src, dst, ss, rs, device):
        return pltpu.make_async_remote_copy(
            src_ref=src, dst_ref=dst, send_sem=ss, recv_sem=rs, device_id=device, device_id_type=MESH
        )

    barrier = pltpu.get_barrier_semaphore()

    def greet(devices):
        for device in devices:
            pl.semaphore_signal(barrier, inc=1, device_id=device, device_id_type=MESH)

    greet([sibling])

    @pl.when(chip > 0)
    def _():
        greet([at(chip - 1, 0), at(chip - 1, 1)])

    @pl.when(chip < last)
    def _():
        greet([at(last, core)])

    @pl.when(chip == last)
    def _():
        def greet_row(i, carry):
            greet([((dp + i) % dp_size, ti)])
            return carry

        lax.fori_loop(1, dp_size, greet_row, 0)

    half = 2 * HEADS * HD
    own_half = pl.ds(pl.multiple_of(core * half, half), half)
    side_half = pl.ds(pl.multiple_of(other * half, half), half)
    own_kv = pl.ds(pl.multiple_of(core * (half // 2), half // 2), half // 2)
    side_kv = pl.ds(pl.multiple_of(other * (half // 2), half // 2), half // 2)
    own_rows = rows_of(2 * CHIP + core * TOK)
    side_rows = rows_of(2 * CHIP + other * TOK)
    loads = [
        pltpu.make_async_copy(k_hbm.at[:, own_kv], kv.at[0, own_rows], load_s.at[0]),
        pltpu.make_async_copy(v_hbm.at[:, own_kv], kv.at[1, own_rows], load_s.at[1]),
        pltpu.make_async_copy(q_hbm.at[:, own_half], qs.at[core], load_s.at[2]),
        pltpu.make_async_copy(g_hbm.at[:, own_half], gs.at[core], load_s.at[3]),
    ]
    small_loads = [
        pltpu.make_async_copy(reward_hbm, reward_ref, small_s.at[0]),
        pltpu.make_async_copy(group_hbm, group_ref, small_s.at[1]),
        pltpu.make_async_copy(keep_hbm, keep_ref, small_s.at[2]),
        pltpu.make_async_copy(dest_hbm, dest_ref, small_s.at[3]),
    ]

    def own_copy(h, i, k):
        src = (k_hbm, v_hbm)[i]
        return remote(
            src.at[:, head_cols(HEADS * k + h)],
            kv.at[i, rows_of(CHIP + core * TOK), head_cols(h)],
            own_ss.at[h, i, k],
            own_rs.at[h, i, core],
            at(chip + 1, k),
        )

    def own_arrival(h, i, k):
        dst = kv.at[i, rows_of(CHIP + k * TOK), head_cols(h)]
        return remote(dst, dst, own_ss.at[h, i, k], own_rs.at[h, i, k], at(chip - 1, k))

    def relay_copy(h, i):
        return remote(
            kv.at[i, pl.ds(CHIP, CHIP), head_cols(h)],
            kv.at[i, pl.ds(0, CHIP), head_cols(h)],
            relay_ss.at[h, i],
            relay_rs.at[h, i],
            at(chip + 1, core),
        )

    def far_copy(h, i):
        return remote(far_out.at[h, i], far_in.at[h, i], far_ss.at[h, i], far_rs.at[h, i], at(chip - 1, core))

    def near_copy(h, i, k):
        return remote(
            near_out.at[h, i, pl.ds(k * TOK, TOK)],
            near_in.at[h, i, core],
            near_ss.at[h, i, k],
            near_rs.at[h, i, core],
            at(chip - 1, k),
        )

    def near_arrival(h, i, k):
        dst = near_in.at[h, i, k]
        return remote(dst, dst, near_ss.at[h, i, k], near_rs.at[h, i, k], at(chip + 1, k))

    def side_copy(h, i):
        return remote(side_out.at[h, i], side_in.at[h, i], side_ss.at[h, i], side_rs.at[h, i], sibling)

    def dq_copy(h):
        return remote(
            dq_side.at[:, head_cols(2 * h, 2)],
            dq_ref.at[:, head_cols(2 * HEADS * core + 2 * h, 2)],
            dq_ss.at[h],
            dq_rs.at[h],
            sibling,
        )

    def dq_arrival(h):
        dst = dq_ref.at[:, head_cols(2 * HEADS * other + 2 * h, 2)]
        return remote(dst, dst, dq_ss.at[h], dq_rs.at[h], sibling)

    def pair_copy(n, rows, place):
        src = (k_hbm, v_hbm, q_hbm, g_hbm)[n].at[:, side_kv if n < 2 else side_half]
        dst = kv.at[n, rows] if n < 2 else (qs, gs)[n - 2].at[place]
        return remote(src, dst, pair_ss.at[n], pair_rs.at[n], sibling)

    def roll_copy(i):
        tile = rolls.at[dp]
        return remote(tile, tile, roll_ss.at[i], roll_rs.at[dp], ((dp + i) % dp_size, ti))

    def roll_arrival(i):
        sender = (dp + dp_size - i) % dp_size
        tile = rolls.at[sender]
        return remote(tile, tile, roll_ss.at[i], roll_rs.at[sender], (sender, ti))

    def every_row(act):
        def step(i, carry):
            act(i)
            return carry

        lax.fori_loop(1, dp_size, step, 0)

    def table_copy(c):
        return remote(table_ref, table_ref, table_ss.at[c], table_rs, at(c, core))

    between = (chip > 0) & (chip < last)

    def next_copy(n, k):
        cols = head_cols(2 * HEADS * k + 2 * MID, 2)
        return remote(
            (q_hbm, g_hbm)[n].at[:, cols],
            q_next.at[n, core],
            next_ss.at[n, k],
            next_rs.at[n, core],
            at(chip - 1, k),
        )

    def next_arrival(n, k):
        dst = q_next.at[n, k]
        return remote(dst, dst, next_ss.at[n, k], next_rs.at[n, k], at(chip + 1, k))

    def stat_down():
        return remote(stat_own, stat_next_in, stat_ss.at[0], stat_rs.at[0], at(chip - 1, core))

    def stat_up():
        return remote(stat_next, stat_own_in, stat_ss.at[1], stat_rs.at[1], at(chip + 1, core))

    def dq_next_copy():
        return remote(dq_next, dq_next_in, dq_next_ss, dq_next_rs, at(chip + 1, core))

    def start_own(h, i):
        for k in range(2):
            own_copy(h, i, k).start()

    def start_pair():
        for n in range(4):
            pair_copy(n, own_rows, core).start()

    @pl.when(chip == last)
    def _():
        for copy in small_loads:
            copy.start()

    @pl.when(chip < last)
    def _():
        pl.semaphore_wait(barrier, 3)
        for n in range(AHEAD):
            start_own(n // 2, n % 2)
        start_pair()

    for copy in loads:
        copy.start()

    @pl.when(chip < 2)
    def _():
        kv[:, 0:CHIP] = jnp.zeros((2, CHIP, HEADS * HD), BF16)

    @pl.when(chip == 0)
    def _():
        kv[:, CHIP : 2 * CHIP] = jnp.zeros((2, CHIP, HEADS * HD), BF16)

    @pl.when(chip < 2)
    def _():
        stat_own_in[...] = jnp.zeros_like(stat_own_in)
        dq_next_in[...] = jnp.zeros_like(dq_next_in)

    @pl.when((chip == 0) | (chip == last))
    def _():
        far_in[...] = jnp.zeros_like(far_in)

    ends = []
    for s in range(SLOTS):
        ends.append(doc_ref[0, s] + (ends[-1] if s else 0))
    for b in range(2):
        query_pos = chip * CHIP + b * TOK + lax.broadcasted_iota(jnp.int32, (1, TOK), 1)
        first = jnp.zeros_like(query_pos)
        for s in range(SLOTS - 1):
            first = jnp.where(query_pos >= ends[s], ends[s], first)
        key_pos = (chip - 2) * CHIP + b * TOK + lax.broadcasted_iota(jnp.int32, (5 * TOK, TOK), 0)
        mask[b] = jnp.where((key_pos <= query_pos) & (key_pos >= first), 1.0, 0.0)
        query_pos = query_pos + CHIP
        first = jnp.zeros_like(query_pos)
        for s in range(SLOTS - 1):
            first = jnp.where(query_pos >= ends[s], ends[s], first)
        key_pos = (chip - 1) * CHIP + lax.broadcasted_iota(jnp.int32, (CHIP, TOK), 0)
        mask_next[b] = jnp.where(key_pos >= first, 1.0, 0.0)

    @pl.when(chip == last)
    def _():
        near_in[...] = jnp.zeros_like(near_in)
        sub = lax.broadcasted_iota(jnp.int32, (8, 128), 0)
        rolls[dp] = jnp.where((sub == 1) | (sub == 3), -1.0, 0.0)
        for copy in small_loads:
            copy.wait()
        rolls[dp, 0:1, 0:ROLL] = reward_ref[...]
        rolls[dp, 1:2, 0:ROLL] = group_ref[...].astype(F32)
        rolls[dp, 2:3, 0:ROLL] = keep_ref[...].astype(F32)
        rolls[dp, 3:4, 0:ROLL] = dest_ref[...].astype(F32)

    def pass_on(h, i):
        @pl.when(chip > 0)
        def _():
            for k in range(2):
                own_arrival(h, i, k).wait_recv()

        @pl.when(between & (h != MID))
        def _():
            relay_copy(h, i).start()

        later, kind = h + (i + AHEAD) // 2, (i + AHEAD) % 2

        @pl.when((chip < last) & (later < HEADS))
        def _():
            start_own(later, kind)

    def stacked(ref, b, h):
        return jnp.concatenate([ref[b, :, head_cols(2 * h)], ref[b, :, head_cols(2 * h + 1)]], axis=0)

    def dot(a, b, dims):
        return lax.dot_general(a, b, (dims, ((), ())), preferred_element_type=F32)

    def share_out(h, i, first, second):
        far_out[h, i, 0:TOK] = first[0:TOK].astype(BF16)
        far_out[h, i, TOK:CHIP] = (first[TOK:CHIP] + second[0:TOK]).astype(BF16)

        @pl.when(chip > 1)
        def _():
            far_copy(h, i).start()

        near[h, i] = first[CHIP : 2 * CHIP] + second[TOK : TOK + CHIP]
        own_part = (first[4 * TOK : 5 * TOK] + second[3 * TOK : 4 * TOK], second[4 * TOK : 5 * TOK])
        mine[h, i] = jnp.where(core == 0, own_part[0], own_part[1])
        side_out[h, i] = jnp.where(core == 0, own_part[1], own_part[0]).astype(BF16)
        side_copy(h, i).start()

    def await_relay(h, i):
        @pl.when(chip > 1)
        def _():
            relay_copy(h, i).wait_recv()

    def with_keys(h):
        await_relay(h, 0)
        value_grads = []
        for b in range(2):
            keys = kv[0, pl.ds(b * TOK, 5 * TOK), head_cols(h)]
            allowed = mask[b]
            capped = jnp.tanh(dot(keys, stacked(qs, b, h), ((1,), (1,))) * to_capped)
            weights = jnp.exp2(capped * to_exponent) * jnp.concatenate([allowed, allowed], axis=1)
            normal = weights * (1.0 / jnp.sum(weights, axis=0, keepdims=True))
            probs[b] = normal
            slope[b] = normal * (1.0 - capped * capped)
            value_grads.append(dot(normal.astype(BF16), stacked(gs, b, h), ((1,), (0,))))
        share_out(h, 1, *value_grads)

    def with_values(h):
        await_relay(h, 1)
        key_grads = []
        for b in range(2):
            window = pl.ds(b * TOK, 5 * TOK)
            prob_grad = dot(kv[1, window, head_cols(h)], stacked(gs, b, h), ((1,), (1,)))
            delta = jnp.sum(probs[b] * prob_grad, axis=0, keepdims=True)
            logit_grad = (slope[b] * (prob_grad - delta)).astype(BF16)
            key_grads.append(dot(logit_grad, stacked(qs, b, h), ((1,), (0,))))
            query_grad = dot(logit_grad, kv[0, window, head_cols(h)], ((0,), (0,)))
            for r in range(2):
                dq_raw[h, b, r] = query_grad[r * TOK : (r + 1) * TOK]
        share_out(h, 0, *key_grads)

    def mid_operands(n):
        _, first, blocks, b = PLACES[n]
        window = pl.ds(first * TOK, blocks * TOK)
        keys, values = kv[0, window, head_cols(MID)], kv[1, window, head_cols(MID)]
        if n < 2:
            return keys, values, stacked(qs, b, MID), stacked(gs, b, MID)
        rows = [jnp.concatenate([q_next[m, b, :, 0:HD], q_next[m, b, :, HD:]], axis=0) for m in range(2)]
        return keys, values, *rows

    def mid_scores(n, allowed):
        keys, values, query, grad = mid_operands(n)
        capped = jnp.tanh(dot(keys, query, ((1,), (1,))) * to_capped)
        weights = jnp.exp2(capped * to_exponent) * jnp.concatenate([allowed, allowed], axis=1)
        prob_grad = dot(values, grad, ((1,), (1,)))
        here = pl.ds(PLACES[n][0] * TOK, PLACES[n][2] * TOK)
        mid_weights[here] = weights
        mid_slope[here] = weights * (1.0 - capped * capped)
        mid_grads[here] = prob_grad
        return [jnp.sum(weights, axis=0, keepdims=True), jnp.sum(weights * prob_grad, axis=0, keepdims=True)]

    def mid_grad(n, stats):
        b = PLACES[n][3]
        inverse = 1.0 / stats[2 * b : 2 * b + 1]
        delta = stats[2 * b + 1 : 2 * b + 2] * inverse
        keys, _, query, grad = mid_operands(n)
        here = pl.ds(PLACES[n][0] * TOK, PLACES[n][2] * TOK)
        logit_grad = (mid_slope[here] * inverse * (mid_grads[here] - delta)).astype(BF16)
        return (
            dot(logit_grad, query, ((1,), (0,))),
            dot((mid_weights[here] * inverse).astype(BF16), grad, ((1,), (0,))),
            dot(logit_grad, keys, ((0,), (0,))),
        )

    def mid_begin():
        stats = mid_scores(0, mask[0, 2 * TOK :]) + mid_scores(1, mask[1, TOK:])
        stat_own[0:4] = jnp.concatenate(stats, axis=0)
        stat_own[4:8] = jnp.zeros((4, 2 * TOK), F32)

        @pl.when(chip > 1)
        def _():
            stat_down().start()

        @pl.when(between)
        def _():
            for n in range(2):
                for k in range(2):
                    next_arrival(n, k).wait_recv()
            stats = mid_scores(2, mask_next[0]) + mid_scores(3, mask_next[1, TOK:])
            stat_next[0:4] = jnp.concatenate(stats, axis=0)
            stat_next[4:8] = jnp.zeros((4, 2 * TOK), F32)
            stat_up().start()

    def mid_end():
        @pl.when(chip > 1)
        def _():
            stat_up().wait_recv()

        stats = stat_own[...] + stat_own_in[...]
        first, second = mid_grad(0, stats), mid_grad(1, stats)
        for i in range(2):
            a, b = first[i], second[i]
            near[MID, i] = a[0:CHIP] + b[0:CHIP]
            own_part = (a[CHIP : 3 * TOK] + b[CHIP : 3 * TOK], b[3 * TOK : 4 * TOK])
            mine[MID, i] = jnp.where(core == 0, own_part[0], own_part[1])
            side_out[MID, i] = jnp.where(core == 0, own_part[1], own_part[0]).astype(BF16)
            side_copy(MID, i).start()
        for b, part in ((0, first[2]), (1, second[2])):
            for r in range(2):
                dq_raw[MID, b, r] = part[r * TOK : (r + 1) * TOK]

        @pl.when(between)
        def _():
            stat_down().wait_recv()
            stats = stat_next[...] + stat_next_in[...]
            first, second = mid_grad(2, stats), mid_grad(3, stats)
            for b, part in ((0, first[2]), (1, second[2])):
                for r in range(2):
                    dq_next[b, r] = part[r * TOK : (r + 1) * TOK].astype(BF16)
            dq_next_copy().start()
            for i in range(2):
                near[MID, i] = near[MID, i] + first[i]
                near[MID, i, TOK:CHIP] = near[MID, i, TOK:CHIP] + second[i]

        @pl.when(chip > 0)
        def _():
            for i in range(2):
                near_out[MID, i] = near[MID, i].astype(BF16)
                for k in range(2):
                    near_copy(MID, i, k).start()

    def pass_back(h, i):
        @pl.when(chip > 0)
        def _():
            @pl.when(chip < last)
            def _():
                far_copy(h, i).wait_recv()

            near_out[h, i] = (near[h, i] + far_in[h, i].astype(F32)).astype(BF16)
            for k in range(2):
                near_copy(h, i, k).start()

    def emit_queries(h):
        if h == MID:

            @pl.when(chip > 1)
            def _():
                dq_next_copy().wait_recv()

        for b, ref, offset in ((core, dq_ref, 2 * HEADS * core), (other, dq_side, 0)):
            scale = weight[1, rows_of(b * TOK)]
            for r in range(2):
                total = dq_raw[h, b, r]
                if h == MID:
                    total = total + dq_next_in[b, r].astype(F32)
                ref[:, head_cols(offset + 2 * h + r)] = (total * scale).astype(BF16)
        dq_copy(h).start()

    def finish(h, i):
        scale = weight[1 - i, rows_of(core * TOK)]
        side_copy(h, i).wait_recv()

        @pl.when(chip < last)
        def _():
            for k in range(2):
                near_arrival(h, i, k).wait_recv()

        a = mine[h, i] + near_in[h, i, core].astype(F32)
        b = side_in[h, i].astype(F32) + near_in[h, i, other].astype(F32)
        result = (dk_ref, dv_ref)[i]
        result[:, head_cols(HEADS * core + h)] = (a * scale).astype(BF16)
        result[:, head_cols(HEADS * other + h)] = (b * scale).astype(BF16)

    def send_rollouts():
        @pl.when(chip == last)
        def _():
            pl.semaphore_wait(barrier, 1 + last + dp_size - 1)
            every_row(lambda i: roll_copy(i).start())

    def make_table():
        @pl.when(chip == last)
        def _():
            every_row(lambda i: roll_arrival(i).wait_recv())
            groups = dp_size * ROLL // GROUP
            table_ref[...] = advantage_table(rolls, groups, dp) + jnp.zeros((SLOTS, 128), F32)
            for c in range(last):
                table_copy(c).start()

    def make_weight():
        @pl.when(chip < last)
        def _():
            remote(table_ref, table_ref, table_ss.at[0], table_rs, at(last, core)).wait_recv()

        token = chip * CHIP + lax.broadcasted_iota(jnp.int32, (CHIP, HD), 0)
        factor = jnp.zeros((CHIP, HD), F32) + table_ref[0:1, :]
        for s in range(1, SLOTS):
            factor = jnp.where(token >= ends[s - 1], table_ref[s : s + 1, :], factor)
        weight[0] = factor
        weight[1] = factor * (1.0 / 12.0)

    pass_on(0, 0)

    @pl.when(chip == last)
    def _():
        start_pair()

    @pl.when(chip > 1)
    def _():
        for n in range(2):
            for k in range(2):
                next_copy(n, k).start()

    pass_on(0, 1)
    for copy in loads:
        copy.wait()
    for n in range(4):
        pair_copy(n, side_rows, other).wait_recv()

    def turn(j, carry):
        h = jnp.where(j == 2, 3, j)

        @pl.when(j < 2)
        def _():
            pass_on(j + 1, 0)

        with_keys(h)

        @pl.when(j > 0)
        def _():
            pass_back(j - 1, 0)

        @pl.when(j == 0)
        def _():
            send_rollouts()

        @pl.when(j < 2)
        def _():
            pass_on(j + 1, 1)

        @pl.when(j == 1)
        def _():
            mid_begin()

        with_values(h)
        pass_back(h, 1)

        @pl.when(j == 1)
        def _():
            pass_on(3, 0)
            pass_on(3, 1)
            mid_end()

        return carry

    lax.fori_loop(0, HEADS - 1, turn, 0)
    pass_back(HEADS - 1, 0)
    make_table()
    make_weight()
    for h in range(HEADS):
        emit_queries(h)
    for h in range(HEADS):
        finish(h, 1)
        finish(h, 0)

    @pl.when(chip == last)
    def _():
        every_row(lambda i: roll_copy(i).wait_send())
        for c in range(last):
            table_copy(c).wait_send()

    for n in range(4):
        pair_copy(n, own_rows, core).wait_send()

    @pl.when(chip > 1)
    def _():
        for n in range(2):
            for k in range(2):
                next_copy(n, k).wait_send()
        stat_down().wait_send()

    @pl.when(between)
    def _():
        stat_up().wait_send()
        dq_next_copy().wait_send()

    def settle(h, carry):
        for i in range(2):
            @pl.when(chip < last)
            def _():
                for k in range(2):
                    own_copy(h, i, k).wait_send()

            @pl.when(chip > 0)
            def _():
                for k in range(2):
                    near_copy(h, i, k).wait_send()

            @pl.when(between & (h != MID))
            def _():
                relay_copy(h, i).wait_send()

            @pl.when((chip > 1) & (h != MID))
            def _():
                far_copy(h, i).wait_send()

            side_copy(h, i).wait_send()
        dq_copy(h).wait_send()
        dq_arrival(h).wait_recv()
        return carry

    lax.fori_loop(0, HEADS, settle, 0)


def hand_over(*refs):
    sources, results, sem = refs[:3], refs[3:6], refs[6]
    copies = [pltpu.make_async_copy(src, dst, sem.at[n]) for n, (src, dst) in enumerate(zip(sources, results))]
    for copy in copies:
        copy.start()
    for copy in copies:
        copy.wait()


def body(reward, group_id, keep, dest, doc_len, query, key, value, grad_out):
    dp_size = lax.axis_size("dp")
    smem = pl.BlockSpec(memory_space=pltpu.SMEM)
    hbm = pl.BlockSpec(memory_space=pl.ANY)
    dma = pltpu.SemaphoreType.DMA
    import_row = lambda a: a.reshape(1, -1)
    half = 2 * HEADS * HD
    shapes = tuple(jax.ShapeDtypeStruct(a.shape, BF16) for a in (query, key, value))
    results = pl.pallas_call(
        kernel,
        out_shape=tuple(pltpu.VMEM(a.shape, BF16) for a in shapes),
        in_specs=[hbm] * 4 + [smem] + [hbm] * 4,
        out_specs=[pl.BlockSpec(memory_space=pltpu.VMEM)] * 3,
        scratch_shapes=[
            pltpu.VMEM((2, 3 * CHIP, HEADS * HD), BF16),
            pltpu.VMEM((2, TOK, half), BF16),
            pltpu.VMEM((2, TOK, half), BF16),
            pltpu.VMEM((2, 5 * TOK, TOK), F32),
            pltpu.VMEM((2, 5 * TOK, 2 * TOK), F32),
            pltpu.VMEM((2, 5 * TOK, 2 * TOK), F32),
            pltpu.VMEM((2, CHIP, HD), F32),
            pltpu.VMEM((1, ROLL), F32),
            pltpu.VMEM((1, ROLL), jnp.int32),
            pltpu.VMEM((1, ROLL), jnp.int32),
            pltpu.VMEM((1, ROLL), jnp.int32),
            pltpu.VMEM((dp_size, 8, 128), F32),
            pltpu.VMEM((SLOTS, 128), F32),
            pltpu.VMEM((2, CHIP, TOK), F32),
            pltpu.VMEM((2, 2, TOK, 2 * HD), BF16),
            pltpu.VMEM((10 * TOK, 2 * TOK), F32),
            pltpu.VMEM((10 * TOK, 2 * TOK), F32),
            pltpu.VMEM((10 * TOK, 2 * TOK), F32),
            pltpu.VMEM((8, 2 * TOK), F32),
            pltpu.VMEM((8, 2 * TOK), F32),
            pltpu.VMEM((8, 2 * TOK), F32),
            pltpu.VMEM((8, 2 * TOK), F32),
            pltpu.VMEM((2, 2, TOK, HD), BF16),
            pltpu.VMEM((2, 2, TOK, HD), BF16),
            pltpu.VMEM((HEADS, 2, CHIP, HD), F32),
            pltpu.VMEM((HEADS, 2, TOK, HD), F32),
            pltpu.VMEM((HEADS, 2, CHIP, HD), BF16),
            pltpu.VMEM((HEADS, 2, CHIP, HD), BF16),
            pltpu.VMEM((HEADS, 2, CHIP, HD), BF16),
            pltpu.VMEM((HEADS, 2, 2, TOK, HD), BF16),
            pltpu.VMEM((HEADS, 2, TOK, HD), BF16),
            pltpu.VMEM((HEADS, 2, TOK, HD), BF16),
            pltpu.VMEM((HEADS, 2, 2, TOK, HD), F32),
            pltpu.VMEM((TOK, half), BF16),
            dma((HEADS, 2, 2)),
            dma((HEADS, 2, 2)),
            dma((HEADS, 2)),
            dma((HEADS, 2)),
            dma((HEADS, 2)),
            dma((HEADS, 2)),
            dma((HEADS, 2, 2)),
            dma((HEADS, 2, 2)),
            dma((HEADS, 2)),
            dma((HEADS, 2)),
            dma((4,)),
            dma((4,)),
            dma((HEADS,)),
            dma((HEADS,)),
            dma((4,)),
            dma((4,)),
            dma((dp_size,)),
            dma((dp_size,)),
            dma((lax.axis_size("tensor") // 2 - 1,)),
            dma,
            dma((2, 2)),
            dma((2, 2)),
            dma((2,)),
            dma((2,)),
            dma,
            dma,
        ],
        compiler_params=pltpu.CompilerParams(
            collective_id=0, has_side_effects=True, vmem_limit_bytes=60 * 1024 * 1024
        ),
        cost_estimate=pl.CostEstimate(flops=2_000_000_000, bytes_accessed=4_000_000, transcendentals=4_000_000),
    )(
        import_row(reward),
        import_row(group_id),
        import_row(keep),
        import_row(dest),
        doc_len,
        *[pltpu.with_memory_space_constraint(a, pltpu.HBM) for a in (query, key, value, grad_out)],
    )
    return pl.pallas_call(
        hand_over,
        out_shape=shapes,
        in_specs=[pl.BlockSpec(memory_space=pltpu.VMEM)] * 3,
        out_specs=[hbm] * 3,
        scratch_shapes=[dma((3,))],
        compiler_params=pltpu.CompilerParams(vmem_limit_bytes=4 * 1024 * 1024),
    )(*[pltpu.with_memory_space_constraint(a, pltpu.VMEM) for a in results])


def solution(mesh):
    return jax.shard_map(
        body,
        mesh=mesh,
        in_specs=(
            P("dp"),
            P("dp"),
            P("dp"),
            P("dp"),
            P("dp", None),
            P(("dp", "tensor"), None),
            P(("dp", "tensor"), None),
            P(("dp", "tensor"), None),
            P(("dp", "tensor"), None),
        ),
        out_specs=(P(("dp", "tensor"), None), P(("dp", "tensor"), None), P(("dp", "tensor"), None)),
        check_vma=False,
    )
```

```python
import math

import jax
import jax.numpy as jnp
from jax import lax
from jax.experimental import pallas as pl
from jax.experimental.pallas import tpu as pltpu
from jax.sharding import PartitionSpec as P

HD = 128
TOK = 128
CHIP = 2 * TOK
SLOTS = 8
GROUP = 16
ROLL = 12
MID = 3
STEPS = (
    "o0 o1 o2 s",
    "o3 p0 q p1",
    "p2 p3 o4 k0",
    "o5 v0 o6 k1",
    "o7 v1 b1 p4",
    "b0 p5 p6 b3",
    "p7 m b2 k2",
    "t v2 e b5",
    "b4",
)
PLACES = ((0, 2, 3, 0), (3, 2, 4, 1), (7, 2, 2, 0), (9, 3, 1, 1))
HEADS = 4
MESH = pl.DeviceIdType.MESH
F32 = jnp.float32
BF16 = jnp.bfloat16

softcap = 50.0
to_capped = 1.0 / (12.0 * softcap)
to_exponent = softcap * math.log2(math.e)


def head_cols(index, width=1):
    return pl.ds(pl.multiple_of(index * HD, HD), width * HD)


def rows_of(start):
    return pl.ds(pl.multiple_of(start, TOK), TOK)


def advantage_table(all_ref, groups, row):
    def field(n):
        return jnp.concatenate([all_ref[i, n : n + 1, :] for i in range(all_ref.shape[0])], axis=0)

    reward, group, keep, dest = field(0), field(1), field(2), field(3)
    counts, sums, squares = [], [], []
    for g in range(groups):
        member = jnp.where(group == float(g), keep, 0.0)
        counts.append(jnp.sum(member, axis=0, keepdims=True))
        sums.append(jnp.sum(member * reward, axis=0, keepdims=True))
        squares.append(jnp.sum(member * reward * reward, axis=0, keepdims=True))

    def total(parts):
        return jnp.sum(jnp.concatenate(parts, axis=0), axis=1, keepdims=True)

    members = jnp.maximum(total(counts), 1.0)
    average = total(sums) / members
    spread = jnp.sqrt(jnp.maximum(total(squares) / members - average * average, 0.0))
    divisor = jnp.maximum(spread, 1.0)
    row_mean = jnp.zeros_like(reward)
    row_divisor = jnp.zeros_like(reward)
    for g in range(groups):
        own = group == float(g)
        row_mean = jnp.where(own, average[g : g + 1, :], row_mean)
        row_divisor = jnp.where(own, divisor[g : g + 1, :], row_divisor)
    row_divisor = jnp.maximum(row_divisor, 1.0)
    advantage = keep * (reward - row_mean) / row_divisor
    slots = []
    for s in range(SLOTS):
        wanted = (row * SLOTS + s).astype(F32)
        slots.append(jnp.sum(jnp.where(dest == wanted, advantage, 0.0), axis=0, keepdims=True))
    return total(slots)


def kernel(
    reward_hbm,
    group_hbm,
    keep_hbm,
    dest_hbm,
    doc_ref,
    q_hbm,
    k_hbm,
    v_hbm,
    g_hbm,
    dq_ref,
    dk_ref,
    dv_ref,
    kv,
    qs,
    gs,
    mask,
    probs,
    slope,
    weight,
    reward_ref,
    group_ref,
    keep_ref,
    dest_ref,
    rolls,
    table_ref,
    mask_next,
    q_next,
    mid_weights,
    mid_slope,
    mid_grads,
    stat_own,
    stat_next,
    stat_own_in,
    stat_next_in,
    dq_next,
    dq_next_in,
    near,
    mine,
    far_out,
    far_in,
    near_out,
    near_in,
    side_out,
    side_in,
    dq_raw,
    dq_side,
    own_ss,
    own_rs,
    relay_ss,
    relay_rs,
    far_ss,
    far_rs,
    near_ss,
    near_rs,
    side_ss,
    side_rs,
    pair_ss,
    pair_rs,
    dq_ss,
    dq_rs,
    load_s,
    small_s,
    roll_ss,
    roll_rs,
    table_ss,
    table_rs,
    next_ss,
    next_rs,
    stat_ss,
    stat_rs,
    dq_next_ss,
    dq_next_rs,
):
    dp = lax.axis_index("dp")
    ti = lax.axis_index("tensor")
    chips = lax.axis_size("tensor") // 2
    dp_size = lax.axis_size("dp")
    chip, core = ti // 2, ti % 2
    other = 1 - core
    last = chips - 1

    def at(c, k):
        return (dp, 2 * c + k)

    sibling = at(chip, other)
    def remote(src, dst, ss, rs, device):
        return pltpu.make_async_remote_copy(
            src_ref=src, dst_ref=dst, send_sem=ss, recv_sem=rs, device_id=device, device_id_type=MESH
        )

    barrier = pltpu.get_barrier_semaphore()

    def greet(devices):
        for device in devices:
            pl.semaphore_signal(barrier, inc=1, device_id=device, device_id_type=MESH)

    greet([sibling])

    @pl.when(chip > 0)
    def _():
        greet([at(chip - 1, 0), at(chip - 1, 1)])

    @pl.when(chip < last)
    def _():
        greet([at(last, core)])

    @pl.when(chip == last)
    def _():
        def greet_row(i, carry):
            greet([((dp + i) % dp_size, ti)])
            return carry

        lax.fori_loop(1, dp_size, greet_row, 0)

    half = 2 * HEADS * HD
    own_half = pl.ds(pl.multiple_of(core * half, half), half)
    side_half = pl.ds(pl.multiple_of(other * half, half), half)
    own_kv = pl.ds(pl.multiple_of(core * (half // 2), half // 2), half // 2)
    side_kv = pl.ds(pl.multiple_of(other * (half // 2), half // 2), half // 2)
    own_rows = rows_of(2 * CHIP + core * TOK)
    side_rows = rows_of(2 * CHIP + other * TOK)
    loads = [
        pltpu.make_async_copy(k_hbm.at[:, own_kv], kv.at[0, own_rows], load_s.at[0]),
        pltpu.make_async_copy(v_hbm.at[:, own_kv], kv.at[1, own_rows], load_s.at[1]),
        pltpu.make_async_copy(q_hbm.at[:, own_half], qs.at[core], load_s.at[2]),
        pltpu.make_async_copy(g_hbm.at[:, own_half], gs.at[core], load_s.at[3]),
    ]
    small_loads = [
        pltpu.make_async_copy(reward_hbm, reward_ref, small_s.at[0]),
        pltpu.make_async_copy(group_hbm, group_ref, small_s.at[1]),
        pltpu.make_async_copy(keep_hbm, keep_ref, small_s.at[2]),
        pltpu.make_async_copy(dest_hbm, dest_ref, small_s.at[3]),
    ]

    def own_copy(h, i, k):
        src = (k_hbm, v_hbm)[i]
        return remote(
            src.at[:, head_cols(HEADS * k + h)],
            kv.at[i, rows_of(CHIP + core * TOK), head_cols(h)],
            own_ss.at[h, i, k],
            own_rs.at[h, i, core],
            at(chip + 1, k),
        )

    def own_arrival(h, i, k):
        dst = kv.at[i, rows_of(CHIP + k * TOK), head_cols(h)]
        return remote(dst, dst, own_ss.at[h, i, k], own_rs.at[h, i, k], at(chip - 1, k))

    def relay_copy(h, i):
        return remote(
            kv.at[i, pl.ds(CHIP, CHIP), head_cols(h)],
            kv.at[i, pl.ds(0, CHIP), head_cols(h)],
            relay_ss.at[h, i],
            relay_rs.at[h, i],
            at(chip + 1, core),
        )

    def far_copy(h, i):
        return remote(far_out.at[h, i], far_in.at[h, i], far_ss.at[h, i], far_rs.at[h, i], at(chip - 1, core))

    def near_copy(h, i, k):
        return remote(
            near_out.at[h, i, pl.ds(k * TOK, TOK)],
            near_in.at[h, i, core],
            near_ss.at[h, i, k],
            near_rs.at[h, i, core],
            at(chip - 1, k),
        )

    def near_arrival(h, i, k):
        dst = near_in.at[h, i, k]
        return remote(dst, dst, near_ss.at[h, i, k], near_rs.at[h, i, k], at(chip + 1, k))

    def side_copy(h, i):
        return remote(side_out.at[h, i], side_in.at[h, i], side_ss.at[h, i], side_rs.at[h, i], sibling)

    def dq_copy(h):
        return remote(
            dq_side.at[:, head_cols(2 * h, 2)],
            dq_ref.at[:, head_cols(2 * HEADS * core + 2 * h, 2)],
            dq_ss.at[h],
            dq_rs.at[h],
            sibling,
        )

    def dq_arrival(h):
        dst = dq_ref.at[:, head_cols(2 * HEADS * other + 2 * h, 2)]
        return remote(dst, dst, dq_ss.at[h], dq_rs.at[h], sibling)

    def pair_copy(n, rows, place):
        src = (k_hbm, v_hbm, q_hbm, g_hbm)[n].at[:, side_kv if n < 2 else side_half]
        dst = kv.at[n, rows] if n < 2 else (qs, gs)[n - 2].at[place]
        return remote(src, dst, pair_ss.at[n], pair_rs.at[n], sibling)

    def roll_copy(i):
        tile = rolls.at[dp]
        return remote(tile, tile, roll_ss.at[i], roll_rs.at[dp], ((dp + i) % dp_size, ti))

    def roll_arrival(i):
        sender = (dp + dp_size - i) % dp_size
        tile = rolls.at[sender]
        return remote(tile, tile, roll_ss.at[i], roll_rs.at[sender], (sender, ti))

    def every_row(act):
        def step(i, carry):
            act(i)
            return carry

        lax.fori_loop(1, dp_size, step, 0)

    def table_copy(c):
        return remote(table_ref, table_ref, table_ss.at[c], table_rs, at(c, core))

    between = (chip > 0) & (chip < last)

    def next_copy(n, k):
        cols = head_cols(2 * HEADS * k + 2 * MID, 2)
        return remote(
            (q_hbm, g_hbm)[n].at[:, cols],
            q_next.at[n, core],
            next_ss.at[n, k],
            next_rs.at[n, core],
            at(chip - 1, k),
        )

    def next_arrival(n, k):
        dst = q_next.at[n, k]
        return remote(dst, dst, next_ss.at[n, k], next_rs.at[n, k], at(chip + 1, k))

    def stat_down():
        return remote(stat_own, stat_next_in, stat_ss.at[0], stat_rs.at[0], at(chip - 1, core))

    def stat_up():
        return remote(stat_next, stat_own_in, stat_ss.at[1], stat_rs.at[1], at(chip + 1, core))

    def dq_next_copy():
        return remote(dq_next, dq_next_in, dq_next_ss, dq_next_rs, at(chip + 1, core))

    def start_own(h, i):
        @pl.when(chip < last)
        def _():
            for k in range(2):
                own_copy(h, i, k).start()

    def start_pair():
        for n in range(4):
            pair_copy(n, own_rows, core).start()

    @pl.when(chip == last)
    def _():
        for copy in small_loads:
            copy.start()

    @pl.when(chip < last)
    def _():
        pl.semaphore_wait(barrier, 3)

    ends = []
    for s in range(SLOTS):
        ends.append(doc_ref[0, s] + (ends[-1] if s else 0))

    def make_masks():
        @pl.when(chip < 2)
        def _():
            kv[:, 0:CHIP] = jnp.zeros((2, CHIP, HEADS * HD), BF16)

        @pl.when(chip == 0)
        def _():
            kv[:, CHIP : 2 * CHIP] = jnp.zeros((2, CHIP, HEADS * HD), BF16)

        @pl.when(chip < 2)
        def _():
            stat_own_in[...] = jnp.zeros_like(stat_own_in)
            dq_next_in[...] = jnp.zeros_like(dq_next_in)

        @pl.when((chip == 0) | (chip == last))
        def _():
            far_in[...] = jnp.zeros_like(far_in)

        for b in range(2):
            query_pos = chip * CHIP + b * TOK + lax.broadcasted_iota(jnp.int32, (1, TOK), 1)
            first = jnp.zeros_like(query_pos)
            for s in range(SLOTS - 1):
                first = jnp.where(query_pos >= ends[s], ends[s], first)
            key_pos = (chip - 2) * CHIP + b * TOK + lax.broadcasted_iota(jnp.int32, (5 * TOK, TOK), 0)
            mask[b] = jnp.where((key_pos <= query_pos) & (key_pos >= first), 1.0, 0.0)
            query_pos = query_pos + CHIP
            first = jnp.zeros_like(query_pos)
            for s in range(SLOTS - 1):
                first = jnp.where(query_pos >= ends[s], ends[s], first)
            key_pos = (chip - 1) * CHIP + lax.broadcasted_iota(jnp.int32, (CHIP, TOK), 0)
            mask_next[b] = jnp.where(key_pos >= first, 1.0, 0.0)

        @pl.when(chip == last)
        def _():
            near_in[...] = jnp.zeros_like(near_in)
            sub = lax.broadcasted_iota(jnp.int32, (8, 128), 0)
            rolls[dp] = jnp.where((sub == 1) | (sub == 3), -1.0, 0.0)
            for copy in small_loads:
                copy.wait()
            rolls[dp, 0:1, 0:ROLL] = reward_ref[...]
            rolls[dp, 1:2, 0:ROLL] = group_ref[...].astype(F32)
            rolls[dp, 2:3, 0:ROLL] = keep_ref[...].astype(F32)
            rolls[dp, 3:4, 0:ROLL] = dest_ref[...].astype(F32)

    def pass_on(h, i):
        @pl.when(chip > 0)
        def _():
            for k in range(2):
                own_arrival(h, i, k).wait_recv()

        @pl.when(between & (h != MID))
        def _():
            relay_copy(h, i).start()

    def stacked(ref, b, h):
        return jnp.concatenate([ref[b, :, head_cols(2 * h)], ref[b, :, head_cols(2 * h + 1)]], axis=0)

    def dot(a, b, dims):
        return lax.dot_general(a, b, (dims, ((), ())), preferred_element_type=F32)

    def share_out(h, i, first, second):
        far_out[h, i, 0:TOK] = first[0:TOK].astype(BF16)
        far_out[h, i, TOK:CHIP] = (first[TOK:CHIP] + second[0:TOK]).astype(BF16)

        @pl.when(chip > 1)
        def _():
            far_copy(h, i).start()

        near[h, i] = first[CHIP : 2 * CHIP] + second[TOK : TOK + CHIP]
        own_part = (first[4 * TOK : 5 * TOK] + second[3 * TOK : 4 * TOK], second[4 * TOK : 5 * TOK])
        mine[h, i] = jnp.where(core == 0, own_part[0], own_part[1])
        side_out[h, i] = jnp.where(core == 0, own_part[1], own_part[0]).astype(BF16)
        side_copy(h, i).start()

    def await_relay(h, i):
        @pl.when(chip > 1)
        def _():
            relay_copy(h, i).wait_recv()

    def with_keys(h):
        await_relay(h, 0)
        value_grads = []
        for b in range(2):
            keys = kv[0, pl.ds(b * TOK, 5 * TOK), head_cols(h)]
            allowed = mask[b]
            capped = jnp.tanh(dot(keys, stacked(qs, b, h), ((1,), (1,))) * to_capped)
            weights = jnp.exp2(capped * to_exponent) * jnp.concatenate([allowed, allowed], axis=1)
            normal = weights * (1.0 / jnp.sum(weights, axis=0, keepdims=True))
            probs[b] = normal
            slope[b] = normal * (1.0 - capped * capped)
            value_grads.append(dot(normal.astype(BF16), stacked(gs, b, h), ((1,), (0,))))
        share_out(h, 1, *value_grads)

    def with_values(h):
        await_relay(h, 1)
        key_grads = []
        for b in range(2):
            window = pl.ds(b * TOK, 5 * TOK)
            prob_grad = dot(kv[1, window, head_cols(h)], stacked(gs, b, h), ((1,), (1,)))
            delta = jnp.sum(probs[b] * prob_grad, axis=0, keepdims=True)
            logit_grad = (slope[b] * (prob_grad - delta)).astype(BF16)
            key_grads.append(dot(logit_grad, stacked(qs, b, h), ((1,), (0,))))
            query_grad = dot(logit_grad, kv[0, window, head_cols(h)], ((0,), (0,)))
            for r in range(2):
                dq_raw[h, b, r] = query_grad[r * TOK : (r + 1) * TOK]
        share_out(h, 0, *key_grads)

    def mid_operands(n):
        _, first, blocks, b = PLACES[n]
        window = pl.ds(first * TOK, blocks * TOK)
        keys, values = kv[0, window, head_cols(MID)], kv[1, window, head_cols(MID)]
        if n < 2:
            return keys, values, stacked(qs, b, MID), stacked(gs, b, MID)
        rows = [jnp.concatenate([q_next[m, b, :, 0:HD], q_next[m, b, :, HD:]], axis=0) for m in range(2)]
        return keys, values, *rows

    def mid_scores(n, allowed):
        keys, values, query, grad = mid_operands(n)
        capped = jnp.tanh(dot(keys, query, ((1,), (1,))) * to_capped)
        weights = jnp.exp2(capped * to_exponent) * jnp.concatenate([allowed, allowed], axis=1)
        prob_grad = dot(values, grad, ((1,), (1,)))
        here = pl.ds(PLACES[n][0] * TOK, PLACES[n][2] * TOK)
        mid_weights[here] = weights
        mid_slope[here] = weights * (1.0 - capped * capped)
        mid_grads[here] = prob_grad
        return [jnp.sum(weights, axis=0, keepdims=True), jnp.sum(weights * prob_grad, axis=0, keepdims=True)]

    def mid_grad(n, stats):
        b = PLACES[n][3]
        inverse = 1.0 / stats[2 * b : 2 * b + 1]
        delta = stats[2 * b + 1 : 2 * b + 2] * inverse
        keys, _, query, grad = mid_operands(n)
        here = pl.ds(PLACES[n][0] * TOK, PLACES[n][2] * TOK)
        logit_grad = (mid_slope[here] * inverse * (mid_grads[here] - delta)).astype(BF16)
        return (
            dot(logit_grad, query, ((1,), (0,))),
            dot((mid_weights[here] * inverse).astype(BF16), grad, ((1,), (0,))),
            dot(logit_grad, keys, ((0,), (0,))),
        )

    def mid_begin():
        stats = mid_scores(0, mask[0, 2 * TOK :]) + mid_scores(1, mask[1, TOK:])
        stat_own[0:4] = jnp.concatenate(stats, axis=0)
        stat_own[4:8] = jnp.zeros((4, 2 * TOK), F32)

        @pl.when(chip > 1)
        def _():
            stat_down().start()

        @pl.when(between)
        def _():
            for n in range(2):
                for k in range(2):
                    next_arrival(n, k).wait_recv()
            stats = mid_scores(2, mask_next[0]) + mid_scores(3, mask_next[1, TOK:])
            stat_next[0:4] = jnp.concatenate(stats, axis=0)
            stat_next[4:8] = jnp.zeros((4, 2 * TOK), F32)
            stat_up().start()

    def mid_end():
        @pl.when(chip > 1)
        def _():
            stat_up().wait_recv()

        stats = stat_own[...] + stat_own_in[...]
        first, second = mid_grad(0, stats), mid_grad(1, stats)
        for i in range(2):
            a, b = first[i], second[i]
            near[MID, i] = a[0:CHIP] + b[0:CHIP]
            own_part = (a[CHIP : 3 * TOK] + b[CHIP : 3 * TOK], b[3 * TOK : 4 * TOK])
            mine[MID, i] = jnp.where(core == 0, own_part[0], own_part[1])
            side_out[MID, i] = jnp.where(core == 0, own_part[1], own_part[0]).astype(BF16)
            side_copy(MID, i).start()
        for b, part in ((0, first[2]), (1, second[2])):
            for r in range(2):
                dq_raw[MID, b, r] = part[r * TOK : (r + 1) * TOK]

        @pl.when(between)
        def _():
            stat_down().wait_recv()
            stats = stat_next[...] + stat_next_in[...]
            first, second = mid_grad(2, stats), mid_grad(3, stats)
            for b, part in ((0, first[2]), (1, second[2])):
                for r in range(2):
                    dq_next[b, r] = part[r * TOK : (r + 1) * TOK].astype(BF16)
            dq_next_copy().start()
            for i in range(2):
                near[MID, i] = near[MID, i] + first[i]
                near[MID, i, TOK:CHIP] = near[MID, i, TOK:CHIP] + second[i]

        @pl.when(chip > 0)
        def _():
            for i in range(2):
                near_out[MID, i] = near[MID, i].astype(BF16)
                for k in range(2):
                    near_copy(MID, i, k).start()

    def pass_back(h, i):
        @pl.when(chip > 0)
        def _():
            @pl.when(chip < last)
            def _():
                far_copy(h, i).wait_recv()

            near_out[h, i] = (near[h, i] + far_in[h, i].astype(F32)).astype(BF16)
            for k in range(2):
                near_copy(h, i, k).start()

    def emit_queries(h):
        if h == MID:

            @pl.when(chip > 1)
            def _():
                dq_next_copy().wait_recv()

        for b, ref, offset in ((core, dq_ref, 2 * HEADS * core), (other, dq_side, 0)):
            scale = weight[1, rows_of(b * TOK)]
            for r in range(2):
                total = dq_raw[h, b, r]
                if h == MID:
                    total = total + dq_next_in[b, r].astype(F32)
                ref[:, head_cols(offset + 2 * h + r)] = (total * scale).astype(BF16)
        dq_copy(h).start()

    def finish(h, i):
        scale = weight[1 - i, rows_of(core * TOK)]
        side_copy(h, i).wait_recv()

        @pl.when(chip < last)
        def _():
            for k in range(2):
                near_arrival(h, i, k).wait_recv()

        a = mine[h, i] + near_in[h, i, core].astype(F32)
        b = side_in[h, i].astype(F32) + near_in[h, i, other].astype(F32)
        result = (dk_ref, dv_ref)[i]
        result[:, head_cols(HEADS * core + h)] = (a * scale).astype(BF16)
        result[:, head_cols(HEADS * other + h)] = (b * scale).astype(BF16)

    def send_rollouts():
        @pl.when(chip == last)
        def _():
            pl.semaphore_wait(barrier, 1 + last + dp_size - 1)
            every_row(lambda i: roll_copy(i).start())

    def make_table():
        @pl.when(chip == last)
        def _():
            every_row(lambda i: roll_arrival(i).wait_recv())
            groups = dp_size * ROLL // GROUP
            table_ref[...] = advantage_table(rolls, groups, dp) + jnp.zeros((SLOTS, 128), F32)
            for c in (last // 2, *range(last // 2 + 1, last), *range(last // 2)):
                table_copy(c).start()

    def make_weight():
        @pl.when(chip < last)
        def _():
            remote(table_ref, table_ref, table_ss.at[0], table_rs, at(last, core)).wait_recv()

        token = chip * CHIP + lax.broadcasted_iota(jnp.int32, (CHIP, HD), 0)
        factor = jnp.zeros((CHIP, HD), F32) + table_ref[0:1, :]
        for s in range(1, SLOTS):
            factor = jnp.where(token >= ends[s - 1], table_ref[s : s + 1, :], factor)
        weight[0] = factor
        weight[1] = factor * (1.0 / 12.0)

    def send_queries():
        @pl.when(chip == last)
        def _():
            start_pair()

        @pl.when(chip > 1)
        def _():
            for n in range(2):
                for k in range(2):
                    next_copy(n, k).start()

    def first_operands():
        for copy in loads:
            copy.wait()
        for n in range(4):
            pair_copy(n, side_rows, other).wait_recv()

    finished = []
    for step in " ".join(STEPS).split():
        kind, unit = step[0], int(step[1:] or 0)
        if kind == "o":
            start_own(unit // 2, unit % 2)
            if unit == 0:
                for copy in loads:
                    copy.start()
            if unit == 1:

                @pl.when(chip < last)
                def _():
                    start_pair()

        elif kind == "s":
            make_masks()
        elif kind == "p":
            pass_on(unit // 2, unit % 2)
        elif kind == "q":
            send_queries()
        elif kind == "k":
            if unit == 0:
                first_operands()
            with_keys(unit)
            if unit == 0:
                send_rollouts()
        elif kind == "v":
            with_values(unit)
        elif kind == "b":
            pass_back(unit // 2, unit % 2)
            finished.append(unit)
        elif kind == "t":
            make_table()
        elif kind == "m":
            mid_begin()
        else:
            mid_end()

    make_weight()
    for h in range(HEADS):
        emit_queries(h)
    for unit in finished[:-2] + [2 * MID + 1, 2 * MID] + finished[-2:]:
        finish(unit // 2, unit % 2)

    @pl.when(chip == last)
    def _():
        every_row(lambda i: roll_copy(i).wait_send())
        for c in range(last):
            table_copy(c).wait_send()

    for n in range(4):
        pair_copy(n, own_rows, core).wait_send()

    @pl.when(chip > 1)
    def _():
        for n in range(2):
            for k in range(2):
                next_copy(n, k).wait_send()
        stat_down().wait_send()

    @pl.when(between)
    def _():
        stat_up().wait_send()
        dq_next_copy().wait_send()

    def settle(h, carry):
        for i in range(2):
            @pl.when(chip < last)
            def _():
                for k in range(2):
                    own_copy(h, i, k).wait_send()

            @pl.when(chip > 0)
            def _():
                for k in range(2):
                    near_copy(h, i, k).wait_send()

            @pl.when(between & (h != MID))
            def _():
                relay_copy(h, i).wait_send()

            @pl.when((chip > 1) & (h != MID))
            def _():
                far_copy(h, i).wait_send()

            side_copy(h, i).wait_send()
        dq_copy(h).wait_send()
        dq_arrival(h).wait_recv()
        return carry

    lax.fori_loop(0, HEADS, settle, 0)


def hand_over(*refs):
    sources, results, sem = refs[:3], refs[3:6], refs[6]
    copies = [pltpu.make_async_copy(src, dst, sem.at[n]) for n, (src, dst) in enumerate(zip(sources, results))]
    for copy in copies:
        copy.start()
    for copy in copies:
        copy.wait()


def body(reward, group_id, keep, dest, doc_len, query, key, value, grad_out):
    dp_size = lax.axis_size("dp")
    smem = pl.BlockSpec(memory_space=pltpu.SMEM)
    hbm = pl.BlockSpec(memory_space=pl.ANY)
    dma = pltpu.SemaphoreType.DMA
    import_row = lambda a: a.reshape(1, -1)
    half = 2 * HEADS * HD
    shapes = tuple(jax.ShapeDtypeStruct(a.shape, BF16) for a in (query, key, value))
    results = pl.pallas_call(
        kernel,
        out_shape=tuple(pltpu.VMEM(a.shape, BF16) for a in shapes),
        in_specs=[hbm] * 4 + [smem] + [hbm] * 4,
        out_specs=[pl.BlockSpec(memory_space=pltpu.VMEM)] * 3,
        scratch_shapes=[
            pltpu.VMEM((2, 3 * CHIP, HEADS * HD), BF16),
            pltpu.VMEM((2, TOK, half), BF16),
            pltpu.VMEM((2, TOK, half), BF16),
            pltpu.VMEM((2, 5 * TOK, TOK), F32),
            pltpu.VMEM((2, 5 * TOK, 2 * TOK), F32),
            pltpu.VMEM((2, 5 * TOK, 2 * TOK), F32),
            pltpu.VMEM((2, CHIP, HD), F32),
            pltpu.VMEM((1, ROLL), F32),
            pltpu.VMEM((1, ROLL), jnp.int32),
            pltpu.VMEM((1, ROLL), jnp.int32),
            pltpu.VMEM((1, ROLL), jnp.int32),
            pltpu.VMEM((dp_size, 8, 128), F32),
            pltpu.VMEM((SLOTS, 128), F32),
            pltpu.VMEM((2, CHIP, TOK), F32),
            pltpu.VMEM((2, 2, TOK, 2 * HD), BF16),
            pltpu.VMEM((10 * TOK, 2 * TOK), F32),
            pltpu.VMEM((10 * TOK, 2 * TOK), F32),
            pltpu.VMEM((10 * TOK, 2 * TOK), F32),
            pltpu.VMEM((8, 2 * TOK), F32),
            pltpu.VMEM((8, 2 * TOK), F32),
            pltpu.VMEM((8, 2 * TOK), F32),
            pltpu.VMEM((8, 2 * TOK), F32),
            pltpu.VMEM((2, 2, TOK, HD), BF16),
            pltpu.VMEM((2, 2, TOK, HD), BF16),
            pltpu.VMEM((HEADS, 2, CHIP, HD), F32),
            pltpu.VMEM((HEADS, 2, TOK, HD), F32),
            pltpu.VMEM((HEADS, 2, CHIP, HD), BF16),
            pltpu.VMEM((HEADS, 2, CHIP, HD), BF16),
            pltpu.VMEM((HEADS, 2, CHIP, HD), BF16),
            pltpu.VMEM((HEADS, 2, 2, TOK, HD), BF16),
            pltpu.VMEM((HEADS, 2, TOK, HD), BF16),
            pltpu.VMEM((HEADS, 2, TOK, HD), BF16),
            pltpu.VMEM((HEADS, 2, 2, TOK, HD), F32),
            pltpu.VMEM((TOK, half), BF16),
            dma((HEADS, 2, 2)),
            dma((HEADS, 2, 2)),
            dma((HEADS, 2)),
            dma((HEADS, 2)),
            dma((HEADS, 2)),
            dma((HEADS, 2)),
            dma((HEADS, 2, 2)),
            dma((HEADS, 2, 2)),
            dma((HEADS, 2)),
            dma((HEADS, 2)),
            dma((4,)),
            dma((4,)),
            dma((HEADS,)),
            dma((HEADS,)),
            dma((4,)),
            dma((4,)),
            dma((dp_size,)),
            dma((dp_size,)),
            dma((lax.axis_size("tensor") // 2 - 1,)),
            dma,
            dma((2, 2)),
            dma((2, 2)),
            dma((2,)),
            dma((2,)),
            dma,
            dma,
        ],
        compiler_params=pltpu.CompilerParams(
            collective_id=0, has_side_effects=True, vmem_limit_bytes=60 * 1024 * 1024
        ),
        cost_estimate=pl.CostEstimate(flops=2_000_000_000, bytes_accessed=4_000_000, transcendentals=4_000_000),
    )(
        import_row(reward),
        import_row(group_id),
        import_row(keep),
        import_row(dest),
        doc_len,
        *[pltpu.with_memory_space_constraint(a, pltpu.HBM) for a in (query, key, value, grad_out)],
    )
    return pl.pallas_call(
        hand_over,
        out_shape=shapes,
        in_specs=[pl.BlockSpec(memory_space=pltpu.VMEM)] * 3,
        out_specs=[hbm] * 3,
        scratch_shapes=[dma((3,))],
        compiler_params=pltpu.CompilerParams(vmem_limit_bytes=4 * 1024 * 1024),
    )(*[pltpu.with_memory_space_constraint(a, pltpu.VMEM) for a in results])


def solution(mesh):
    return jax.shard_map(
        body,
        mesh=mesh,
        in_specs=(
            P("dp"),
            P("dp"),
            P("dp"),
            P("dp"),
            P("dp", None),
            P(("dp", "tensor"), None),
            P(("dp", "tensor"), None),
            P(("dp", "tensor"), None),
            P(("dp", "tensor"), None),
        ),
        out_specs=(P(("dp", "tensor"), None), P(("dp", "tensor"), None), P(("dp", "tensor"), None)),
        check_vma=False,
    )
```

```python
import math

import jax
import jax.numpy as jnp
from jax import lax
from jax.experimental import pallas as pl
from jax.experimental.pallas import tpu as pltpu
from jax.sharding import PartitionSpec as P

HD = 128
TOK = 128
CHIP = 2 * TOK
SLOTS = 8
GROUP = 16
ROLL = 12
MID = 3
STEPS = (
    "o0 o1 o2 s",
    "o3 p0 q p1",
    "p2 p3 o4 k0",
    "o5 v0 o6 k1",
    "o7 v1 b1 p4",
    "b0 p5 p6 b3",
    "p7 m b2 k2",
    "t v2 e b5",
    "b4",
)
PLACES = ((0, 2, 3, 0), (3, 2, 4, 1), (7, 2, 2, 0), (9, 3, 1, 1))
HEADS = 4
MESH = pl.DeviceIdType.MESH
F32 = jnp.float32
BF16 = jnp.bfloat16

softcap = 50.0
to_capped = 1.0 / (12.0 * softcap)
to_exponent = softcap * math.log2(math.e)


def head_cols(index, width=1):
    return pl.ds(pl.multiple_of(index * HD, HD), width * HD)


def rows_of(start):
    return pl.ds(pl.multiple_of(start, TOK), TOK)


def advantage_table(all_ref, groups, row):
    def field(n):
        return jnp.concatenate([all_ref[i, n : n + 1, :] for i in range(all_ref.shape[0])], axis=0)

    reward, group, keep, dest = field(0), field(1), field(2), field(3)
    counts, sums, squares = [], [], []
    for g in range(groups):
        member = jnp.where(group == float(g), keep, 0.0)
        counts.append(jnp.sum(member, axis=0, keepdims=True))
        sums.append(jnp.sum(member * reward, axis=0, keepdims=True))
        squares.append(jnp.sum(member * reward * reward, axis=0, keepdims=True))

    def total(parts):
        return jnp.sum(jnp.concatenate(parts, axis=0), axis=1, keepdims=True)

    members = jnp.maximum(total(counts), 1.0)
    average = total(sums) / members
    spread = jnp.sqrt(jnp.maximum(total(squares) / members - average * average, 0.0))
    divisor = jnp.maximum(spread, 1.0)
    row_mean = jnp.zeros_like(reward)
    row_divisor = jnp.zeros_like(reward)
    for g in range(groups):
        own = group == float(g)
        row_mean = jnp.where(own, average[g : g + 1, :], row_mean)
        row_divisor = jnp.where(own, divisor[g : g + 1, :], row_divisor)
    row_divisor = jnp.maximum(row_divisor, 1.0)
    advantage = keep * (reward - row_mean) / row_divisor
    slots = []
    for s in range(SLOTS):
        wanted = (row * SLOTS + s).astype(F32)
        slots.append(jnp.sum(jnp.where(dest == wanted, advantage, 0.0), axis=0, keepdims=True))
    return total(slots)


def kernel(
    reward_hbm,
    group_hbm,
    keep_hbm,
    dest_hbm,
    doc_ref,
    q_hbm,
    k_hbm,
    v_hbm,
    g_hbm,
    dq_ref,
    dk_ref,
    dv_ref,
    kv,
    qs,
    gs,
    mask,
    probs,
    slope,
    weight,
    reward_ref,
    group_ref,
    keep_ref,
    dest_ref,
    rolls,
    table_ref,
    mask_next,
    q_next,
    mid_weights,
    mid_slope,
    mid_grads,
    stat_own,
    stat_next,
    stat_own_in,
    stat_next_in,
    dq_next,
    dq_next_in,
    near,
    mine,
    far_out,
    far_in,
    near_out,
    near_in,
    side_out,
    side_in,
    dq_raw,
    dq_side,
    own_ss,
    own_rs,
    relay_ss,
    relay_rs,
    far_ss,
    far_rs,
    near_ss,
    near_rs,
    side_ss,
    side_rs,
    pair_ss,
    pair_rs,
    dq_ss,
    dq_rs,
    load_s,
    small_s,
    roll_ss,
    roll_rs,
    table_ss,
    table_rs,
    next_ss,
    next_rs,
    stat_ss,
    stat_rs,
    dq_next_ss,
    dq_next_rs,
):
    dp = lax.axis_index("dp")
    ti = lax.axis_index("tensor")
    chips = lax.axis_size("tensor") // 2
    dp_size = lax.axis_size("dp")
    chip, core = ti // 2, ti % 2
    other = 1 - core
    last = chips - 1

    def at(c, k):
        return (dp, 2 * c + k)

    sibling = at(chip, other)
    def remote(src, dst, ss, rs, device):
        return pltpu.make_async_remote_copy(
            src_ref=src, dst_ref=dst, send_sem=ss, recv_sem=rs, device_id=device, device_id_type=MESH
        )

    barrier = pltpu.get_barrier_semaphore()

    def greet(devices):
        for device in devices:
            pl.semaphore_signal(barrier, inc=1, device_id=device, device_id_type=MESH)

    greet([sibling])

    @pl.when(chip > 0)
    def _():
        greet([at(chip - 1, 0), at(chip - 1, 1)])

    @pl.when(chip < last)
    def _():
        greet([at(last, core)])

    @pl.when(chip == last)
    def _():
        def greet_row(i, carry):
            greet([((dp + i) % dp_size, ti)])
            return carry

        lax.fori_loop(1, dp_size, greet_row, 0)

    half = 2 * HEADS * HD
    own_half = pl.ds(pl.multiple_of(core * half, half), half)
    side_half = pl.ds(pl.multiple_of(other * half, half), half)
    own_kv = pl.ds(pl.multiple_of(core * (half // 2), half // 2), half // 2)
    side_kv = pl.ds(pl.multiple_of(other * (half // 2), half // 2), half // 2)
    own_rows = rows_of(2 * CHIP + core * TOK)
    side_rows = rows_of(2 * CHIP + other * TOK)
    loads = [
        pltpu.make_async_copy(k_hbm.at[:, own_kv], kv.at[0, own_rows], load_s.at[0]),
        pltpu.make_async_copy(v_hbm.at[:, own_kv], kv.at[1, own_rows], load_s.at[1]),
        pltpu.make_async_copy(q_hbm.at[:, own_half], qs.at[core], load_s.at[2]),
        pltpu.make_async_copy(g_hbm.at[:, own_half], gs.at[core], load_s.at[3]),
    ]
    small_loads = [
        pltpu.make_async_copy(reward_hbm, reward_ref, small_s.at[0]),
        pltpu.make_async_copy(group_hbm, group_ref, small_s.at[1]),
        pltpu.make_async_copy(keep_hbm, keep_ref, small_s.at[2]),
        pltpu.make_async_copy(dest_hbm, dest_ref, small_s.at[3]),
    ]

    def own_copy(h, i, k):
        src = (k_hbm, v_hbm)[i]
        return remote(
            src.at[:, head_cols(HEADS * k + h)],
            kv.at[i, rows_of(CHIP + core * TOK), head_cols(h)],
            own_ss.at[h, i, k],
            own_rs.at[h, i, core],
            at(chip + 1, k),
        )

    def own_arrival(h, i, k):
        dst = kv.at[i, rows_of(CHIP + k * TOK), head_cols(h)]
        return remote(dst, dst, own_ss.at[h, i, k], own_rs.at[h, i, k], at(chip - 1, k))

    def relay_copy(h, i):
        return remote(
            kv.at[i, pl.ds(CHIP, CHIP), head_cols(h)],
            kv.at[i, pl.ds(0, CHIP), head_cols(h)],
            relay_ss.at[h, i],
            relay_rs.at[h, i],
            at(chip + 1, core),
        )

    def relay_arrival(h, i):
        dst = kv.at[i, pl.ds(0, CHIP), head_cols(h)]
        return remote(dst, dst, relay_ss.at[h, i], relay_rs.at[h, i], at(chip - 1, core))

    def far_copy(h, i):
        return remote(far_out.at[h, i], far_in.at[h, i], far_ss.at[h, i], far_rs.at[h, i], at(chip - 1, core))

    def near_copy(h, i, k):
        return remote(
            near_out.at[h, i, pl.ds(k * TOK, TOK)],
            near_in.at[h, i, core],
            near_ss.at[h, i, k],
            near_rs.at[h, i, core],
            at(chip - 1, k),
        )

    def near_arrival(h, i, k):
        dst = near_in.at[h, i, k]
        return remote(dst, dst, near_ss.at[h, i, k], near_rs.at[h, i, k], at(chip + 1, k))

    def side_copy(h, i):
        return remote(side_out.at[h, i], side_in.at[h, i], side_ss.at[h, i], side_rs.at[h, i], sibling)

    def dq_copy(h):
        return remote(
            dq_side.at[:, head_cols(2 * h, 2)],
            dq_ref.at[:, head_cols(2 * HEADS * core + 2 * h, 2)],
            dq_ss.at[h],
            dq_rs.at[h],
            sibling,
        )

    def dq_arrival(h):
        dst = dq_ref.at[:, head_cols(2 * HEADS * other + 2 * h, 2)]
        return remote(dst, dst, dq_ss.at[h], dq_rs.at[h], sibling)

    def pair_copy(n, rows, place):
        src = (k_hbm, v_hbm, q_hbm, g_hbm)[n].at[:, side_kv if n < 2 else side_half]
        dst = kv.at[n, rows] if n < 2 else (qs, gs)[n - 2].at[place]
        return remote(src, dst, pair_ss.at[n], pair_rs.at[n], sibling)

    def roll_copy(i):
        tile = rolls.at[dp]
        return remote(tile, tile, roll_ss.at[i], roll_rs.at[dp], ((dp + i) % dp_size, ti))

    def roll_arrival(i):
        sender = (dp + dp_size - i) % dp_size
        tile = rolls.at[sender]
        return remote(tile, tile, roll_ss.at[i], roll_rs.at[sender], (sender, ti))

    def every_row(act):
        def step(i, carry):
            act(i)
            return carry

        lax.fori_loop(1, dp_size, step, 0)

    def table_copy(c):
        return remote(table_ref, table_ref, table_ss.at[c], table_rs, at(c, core))

    between = (chip > 0) & (chip < last)

    def next_copy(n, k):
        cols = head_cols(2 * HEADS * k + 2 * MID, 2)
        return remote(
            (q_hbm, g_hbm)[n].at[:, cols],
            q_next.at[n, core],
            next_ss.at[n, k],
            next_rs.at[n, core],
            at(chip - 1, k),
        )

    def next_arrival(n, k):
        dst = q_next.at[n, k]
        return remote(dst, dst, next_ss.at[n, k], next_rs.at[n, k], at(chip + 1, k))

    def stat_down():
        return remote(stat_own, stat_next_in, stat_ss.at[0], stat_rs.at[0], at(chip - 1, core))

    def stat_up():
        return remote(stat_next, stat_own_in, stat_ss.at[1], stat_rs.at[1], at(chip + 1, core))

    def stat_arrival():
        return remote(stat_own_in, stat_own_in, stat_ss.at[1], stat_rs.at[1], at(chip - 1, core))

    def dq_next_arrival():
        return remote(dq_next_in, dq_next_in, dq_next_ss, dq_next_rs, at(chip - 1, core))

    def dq_next_copy():
        return remote(dq_next, dq_next_in, dq_next_ss, dq_next_rs, at(chip + 1, core))

    def start_own(h, i):
        @pl.when(chip < last)
        def _():
            for k in range(2):
                own_copy(h, i, k).start()

    def start_pair():
        for n in range(4):
            pair_copy(n, own_rows, core).start()

    @pl.when(chip == last)
    def _():
        for copy in small_loads:
            copy.start()

    @pl.when(chip < last)
    def _():
        pl.semaphore_wait(barrier, 3)

    ends = []
    for s in range(SLOTS):
        ends.append(doc_ref[0, s] + (ends[-1] if s else 0))

    def make_masks():
        @pl.when(chip < 2)
        def _():
            kv[:, 0:CHIP] = jnp.zeros((2, CHIP, HEADS * HD), BF16)

        @pl.when(chip == 0)
        def _():
            kv[:, CHIP : 2 * CHIP] = jnp.zeros((2, CHIP, HEADS * HD), BF16)

        @pl.when(chip < 2)
        def _():
            stat_own_in[...] = jnp.zeros_like(stat_own_in)
            dq_next_in[...] = jnp.zeros_like(dq_next_in)

        @pl.when((chip == 0) | (chip == last))
        def _():
            far_in[...] = jnp.zeros_like(far_in)

        for b in range(2):
            query_pos = chip * CHIP + b * TOK + lax.broadcasted_iota(jnp.int32, (1, TOK), 1)
            first = jnp.zeros_like(query_pos)
            for s in range(SLOTS - 1):
                first = jnp.where(query_pos >= ends[s], ends[s], first)
            key_pos = (chip - 2) * CHIP + b * TOK + lax.broadcasted_iota(jnp.int32, (5 * TOK, TOK), 0)
            mask[b] = jnp.where((key_pos <= query_pos) & (key_pos >= first), 1.0, 0.0)
            query_pos = query_pos + CHIP
            first = jnp.zeros_like(query_pos)
            for s in range(SLOTS - 1):
                first = jnp.where(query_pos >= ends[s], ends[s], first)
            key_pos = (chip - 1) * CHIP + lax.broadcasted_iota(jnp.int32, (CHIP, TOK), 0)
            mask_next[b] = jnp.where(key_pos >= first, 1.0, 0.0)

        @pl.when(chip == last)
        def _():
            near_in[...] = jnp.zeros_like(near_in)
            sub = lax.broadcasted_iota(jnp.int32, (8, 128), 0)
            rolls[dp] = jnp.where((sub == 1) | (sub == 3), -1.0, 0.0)
            for copy in small_loads:
                copy.wait()
            rolls[dp, 0:1, 0:ROLL] = reward_ref[...]
            rolls[dp, 1:2, 0:ROLL] = group_ref[...].astype(F32)
            rolls[dp, 2:3, 0:ROLL] = keep_ref[...].astype(F32)
            rolls[dp, 3:4, 0:ROLL] = dest_ref[...].astype(F32)

    def pass_on(h, i):
        @pl.when(chip > 0)
        def _():
            for k in range(2):
                own_arrival(h, i, k).wait_recv()

        @pl.when(between & (h != MID))
        def _():
            relay_copy(h, i).start()

    def stacked(ref, b, h):
        return jnp.concatenate([ref[b, :, head_cols(2 * h)], ref[b, :, head_cols(2 * h + 1)]], axis=0)

    def dot(a, b, dims):
        return lax.dot_general(a, b, (dims, ((), ())), preferred_element_type=F32)

    def share_out(h, i, first, second):
        far_out[h, i, 0:TOK] = first[0:TOK].astype(BF16)
        far_out[h, i, TOK:CHIP] = (first[TOK:CHIP] + second[0:TOK]).astype(BF16)

        @pl.when(chip > 1)
        def _():
            far_copy(h, i).start()

        near[h, i] = first[CHIP : 2 * CHIP] + second[TOK : TOK + CHIP]
        own_part = (first[4 * TOK : 5 * TOK] + second[3 * TOK : 4 * TOK], second[4 * TOK : 5 * TOK])
        mine[h, i] = jnp.where(core == 0, own_part[0], own_part[1])
        side_out[h, i] = jnp.where(core == 0, own_part[1], own_part[0]).astype(BF16)
        side_copy(h, i).start()

    def await_relay(h, i):
        @pl.when(chip > 1)
        def _():
            relay_arrival(h, i).wait_recv()

    def with_keys(h):
        await_relay(h, 0)
        value_grads, kept = [], []
        for b in range(2):
            keys = kv[0, pl.ds(b * TOK, 5 * TOK), head_cols(h)]
            allowed = mask[b]
            capped = jnp.tanh(dot(keys, stacked(qs, b, h), ((1,), (1,))) * to_capped)
            weights = jnp.exp2(capped * to_exponent) * jnp.concatenate([allowed, allowed], axis=1)
            normal = weights * (1.0 / jnp.sum(weights, axis=0, keepdims=True))
            kept.append((normal, capped))
            value_grads.append(dot(normal.astype(BF16), stacked(gs, b, h), ((1,), (0,))))
        share_out(h, 1, *value_grads)
        for b, (normal, capped) in enumerate(kept):
            probs[b] = normal
            slope[b] = normal * (1.0 - capped * capped)

    def with_values(h):
        await_relay(h, 1)
        key_grads, kept = [], []
        for b in range(2):
            window = pl.ds(b * TOK, 5 * TOK)
            prob_grad = dot(kv[1, window, head_cols(h)], stacked(gs, b, h), ((1,), (1,)))
            delta = jnp.sum(probs[b] * prob_grad, axis=0, keepdims=True)
            logit_grad = (slope[b] * (prob_grad - delta)).astype(BF16)
            key_grads.append(dot(logit_grad, stacked(qs, b, h), ((1,), (0,))))
            kept.append(logit_grad)
        share_out(h, 0, *key_grads)
        for b, logit_grad in enumerate(kept):
            query_grad = dot(logit_grad, kv[0, pl.ds(b * TOK, 5 * TOK), head_cols(h)], ((0,), (0,)))
            for r in range(2):
                dq_raw[h, b, r] = query_grad[r * TOK : (r + 1) * TOK]

    def mid_operands(n):
        _, first, blocks, b = PLACES[n]
        window = pl.ds(first * TOK, blocks * TOK)
        keys, values = kv[0, window, head_cols(MID)], kv[1, window, head_cols(MID)]
        if n < 2:
            return keys, values, stacked(qs, b, MID), stacked(gs, b, MID)
        rows = [jnp.concatenate([q_next[m, b, :, 0:HD], q_next[m, b, :, HD:]], axis=0) for m in range(2)]
        return keys, values, *rows

    def mid_scores(n, allowed):
        keys, values, query, grad = mid_operands(n)
        capped = jnp.tanh(dot(keys, query, ((1,), (1,))) * to_capped)
        weights = jnp.exp2(capped * to_exponent) * jnp.concatenate([allowed, allowed], axis=1)
        prob_grad = dot(values, grad, ((1,), (1,)))
        here = pl.ds(PLACES[n][0] * TOK, PLACES[n][2] * TOK)
        mid_weights[here] = weights
        mid_slope[here] = weights * (1.0 - capped * capped)
        mid_grads[here] = prob_grad
        return [jnp.sum(weights, axis=0, keepdims=True), jnp.sum(weights * prob_grad, axis=0, keepdims=True)]

    def mid_grad(n, stats):
        b = PLACES[n][3]
        inverse = 1.0 / stats[2 * b : 2 * b + 1]
        delta = stats[2 * b + 1 : 2 * b + 2] * inverse
        keys, _, query, grad = mid_operands(n)
        here = pl.ds(PLACES[n][0] * TOK, PLACES[n][2] * TOK)
        logit_grad = (mid_slope[here] * inverse * (mid_grads[here] - delta)).astype(BF16)
        return (
            dot(logit_grad, query, ((1,), (0,))),
            dot((mid_weights[here] * inverse).astype(BF16), grad, ((1,), (0,))),
            dot(logit_grad, keys, ((0,), (0,))),
        )

    def mid_begin():
        stats = mid_scores(0, mask[0, 2 * TOK :]) + mid_scores(1, mask[1, TOK:])
        stat_own[0:4] = jnp.concatenate(stats, axis=0)
        stat_own[4:8] = jnp.zeros((4, 2 * TOK), F32)

        @pl.when(chip > 1)
        def _():
            stat_down().start()

        @pl.when(between)
        def _():
            for n in range(2):
                for k in range(2):
                    next_arrival(n, k).wait_recv()
            stats = mid_scores(2, mask_next[0]) + mid_scores(3, mask_next[1, TOK:])
            stat_next[0:4] = jnp.concatenate(stats, axis=0)
            stat_next[4:8] = jnp.zeros((4, 2 * TOK), F32)
            stat_up().start()

    def mid_end():
        @pl.when(chip > 1)
        def _():
            stat_arrival().wait_recv()

        stats = stat_own[...] + stat_own_in[...]
        first, second = mid_grad(0, stats), mid_grad(1, stats)
        for i in range(2):
            a, b = first[i], second[i]
            near[MID, i] = a[0:CHIP] + b[0:CHIP]
            own_part = (a[CHIP : 3 * TOK] + b[CHIP : 3 * TOK], b[3 * TOK : 4 * TOK])
            mine[MID, i] = jnp.where(core == 0, own_part[0], own_part[1])
            side_out[MID, i] = jnp.where(core == 0, own_part[1], own_part[0]).astype(BF16)
            side_copy(MID, i).start()
        for b, part in ((0, first[2]), (1, second[2])):
            for r in range(2):
                dq_raw[MID, b, r] = part[r * TOK : (r + 1) * TOK]

        @pl.when(between)
        def _():
            stat_down().wait_recv()
            stats = stat_next[...] + stat_next_in[...]
            first, second = mid_grad(2, stats), mid_grad(3, stats)
            for b, part in ((0, first[2]), (1, second[2])):
                for r in range(2):
                    dq_next[b, r] = part[r * TOK : (r + 1) * TOK].astype(BF16)
            dq_next_copy().start()
            for i in range(2):
                near[MID, i] = near[MID, i] + first[i]
                near[MID, i, TOK:CHIP] = near[MID, i, TOK:CHIP] + second[i]

        @pl.when(chip > 0)
        def _():
            for i in range(2):
                near_out[MID, i] = near[MID, i].astype(BF16)
                for k in range(2):
                    near_copy(MID, i, k).start()

    def pass_back(h, i):
        @pl.when(chip > 0)
        def _():
            @pl.when(chip < last)
            def _():
                far_copy(h, i).wait_recv()

            near_out[h, i] = (near[h, i] + far_in[h, i].astype(F32)).astype(BF16)
            for k in range(2):
                near_copy(h, i, k).start()

    def emit_queries(h):
        if h == MID:

            @pl.when(chip > 1)
            def _():
                dq_next_arrival().wait_recv()

        for b, ref, offset in ((core, dq_ref, 2 * HEADS * core), (other, dq_side, 0)):
            scale = weight[1, rows_of(b * TOK)]
            for r in range(2):
                total = dq_raw[h, b, r]
                if h == MID:
                    total = total + dq_next_in[b, r].astype(F32)
                ref[:, head_cols(offset + 2 * h + r)] = (total * scale).astype(BF16)
        dq_copy(h).start()

    def finish(h, i):
        scale = weight[1 - i, rows_of(core * TOK)]
        side_copy(h, i).wait_recv()

        @pl.when(chip < last)
        def _():
            for k in range(2):
                near_arrival(h, i, k).wait_recv()

        a = mine[h, i] + near_in[h, i, core].astype(F32)
        b = side_in[h, i].astype(F32) + near_in[h, i, other].astype(F32)
        result = (dk_ref, dv_ref)[i]
        result[:, head_cols(HEADS * core + h)] = (a * scale).astype(BF16)
        result[:, head_cols(HEADS * other + h)] = (b * scale).astype(BF16)

    def send_rollouts():
        @pl.when(chip == last)
        def _():
            pl.semaphore_wait(barrier, 1 + last + dp_size - 1)
            every_row(lambda i: roll_copy(i).start())

    def make_table():
        @pl.when(chip == last)
        def _():
            every_row(lambda i: roll_arrival(i).wait_recv())
            groups = dp_size * ROLL // GROUP
            table_ref[...] = advantage_table(rolls, groups, dp) + jnp.zeros((SLOTS, 128), F32)
            for c in (last // 2, *range(last // 2 + 1, last), *range(last // 2)):
                table_copy(c).start()

    def make_weight():
        @pl.when(chip < last)
        def _():
            remote(table_ref, table_ref, table_ss.at[0], table_rs, at(last, core)).wait_recv()

        token = chip * CHIP + lax.broadcasted_iota(jnp.int32, (CHIP, HD), 0)
        factor = jnp.zeros((CHIP, HD), F32) + table_ref[0:1, :]
        for s in range(1, SLOTS):
            factor = jnp.where(token >= ends[s - 1], table_ref[s : s + 1, :], factor)
        weight[0] = factor
        weight[1] = factor * (1.0 / 12.0)

    def send_queries():
        @pl.when(chip == last)
        def _():
            start_pair()

        @pl.when(chip > 1)
        def _():
            for n in range(2):
                for k in range(2):
                    next_copy(n, k).start()

    def first_operands():
        for copy in loads:
            copy.wait()
        for n in range(4):
            pair_copy(n, side_rows, other).wait_recv()

    finished = []
    for step in " ".join(STEPS).split():
        kind, unit = step[0], int(step[1:] or 0)
        if kind == "o":
            start_own(unit // 2, unit % 2)
            if unit == 0:
                for copy in loads:
                    copy.start()
            if unit == 1:

                @pl.when(chip < last)
                def _():
                    start_pair()

        elif kind == "s":
            make_masks()
        elif kind == "p":
            pass_on(unit // 2, unit % 2)
        elif kind == "q":
            send_queries()
        elif kind == "k":
            if unit == 0:
                first_operands()
            with_keys(unit)
            if unit == 0:
                send_rollouts()
        elif kind == "v":
            with_values(unit)
        elif kind == "b":
            pass_back(unit // 2, unit % 2)
            finished.append(unit)
        elif kind == "t":
            make_table()
        elif kind == "m":
            mid_begin()
        else:
            mid_end()

    make_weight()
    for h in range(HEADS):
        emit_queries(h)
    for unit in finished[:-2] + [2 * MID + 1, 2 * MID] + finished[-2:]:
        finish(unit // 2, unit % 2)

    @pl.when(chip == last)
    def _():
        every_row(lambda i: roll_copy(i).wait_send())
        for c in range(last):
            table_copy(c).wait_send()

    for n in range(4):
        pair_copy(n, own_rows, core).wait_send()

    @pl.when(chip > 1)
    def _():
        for n in range(2):
            for k in range(2):
                next_copy(n, k).wait_send()
        stat_down().wait_send()

    @pl.when(between)
    def _():
        stat_up().wait_send()
        dq_next_copy().wait_send()

    def settle(h, carry):
        for i in range(2):
            @pl.when(chip < last)
            def _():
                for k in range(2):
                    own_copy(h, i, k).wait_send()

            @pl.when(chip > 0)
            def _():
                for k in range(2):
                    near_copy(h, i, k).wait_send()

            @pl.when(between & (h != MID))
            def _():
                relay_copy(h, i).wait_send()

            @pl.when((chip > 1) & (h != MID))
            def _():
                far_copy(h, i).wait_send()

            side_copy(h, i).wait_send()
        dq_copy(h).wait_send()
        dq_arrival(h).wait_recv()
        return carry

    lax.fori_loop(0, HEADS, settle, 0)


def hand_over(*refs):
    sources, results, sem = refs[:3], refs[3:6], refs[6]
    copies = [pltpu.make_async_copy(src, dst, sem.at[n]) for n, (src, dst) in enumerate(zip(sources, results))]
    for copy in copies:
        copy.start()
    for copy in copies:
        copy.wait()


def body(reward, group_id, keep, dest, doc_len, query, key, value, grad_out):
    dp_size = lax.axis_size("dp")
    smem = pl.BlockSpec(memory_space=pltpu.SMEM)
    hbm = pl.BlockSpec(memory_space=pl.ANY)
    dma = pltpu.SemaphoreType.DMA
    import_row = lambda a: a.reshape(1, -1)
    half = 2 * HEADS * HD
    shapes = tuple(jax.ShapeDtypeStruct(a.shape, BF16) for a in (query, key, value))
    results = pl.pallas_call(
        kernel,
        out_shape=tuple(pltpu.VMEM(a.shape, BF16) for a in shapes),
        in_specs=[hbm] * 4 + [smem] + [hbm] * 4,
        out_specs=[pl.BlockSpec(memory_space=pltpu.VMEM)] * 3,
        scratch_shapes=[
            pltpu.VMEM((2, 3 * CHIP, HEADS * HD), BF16),
            pltpu.VMEM((2, TOK, half), BF16),
            pltpu.VMEM((2, TOK, half), BF16),
            pltpu.VMEM((2, 5 * TOK, TOK), F32),
            pltpu.VMEM((2, 5 * TOK, 2 * TOK), F32),
            pltpu.VMEM((2, 5 * TOK, 2 * TOK), F32),
            pltpu.VMEM((2, CHIP, HD), F32),
            pltpu.VMEM((1, ROLL), F32),
            pltpu.VMEM((1, ROLL), jnp.int32),
            pltpu.VMEM((1, ROLL), jnp.int32),
            pltpu.VMEM((1, ROLL), jnp.int32),
            pltpu.VMEM((dp_size, 8, 128), F32),
            pltpu.VMEM((SLOTS, 128), F32),
            pltpu.VMEM((2, CHIP, TOK), F32),
            pltpu.VMEM((2, 2, TOK, 2 * HD), BF16),
            pltpu.VMEM((10 * TOK, 2 * TOK), F32),
            pltpu.VMEM((10 * TOK, 2 * TOK), F32),
            pltpu.VMEM((10 * TOK, 2 * TOK), F32),
            pltpu.VMEM((8, 2 * TOK), F32),
            pltpu.VMEM((8, 2 * TOK), F32),
            pltpu.VMEM((8, 2 * TOK), F32),
            pltpu.VMEM((8, 2 * TOK), F32),
            pltpu.VMEM((2, 2, TOK, HD), BF16),
            pltpu.VMEM((2, 2, TOK, HD), BF16),
            pltpu.VMEM((HEADS, 2, CHIP, HD), F32),
            pltpu.VMEM((HEADS, 2, TOK, HD), F32),
            pltpu.VMEM((HEADS, 2, CHIP, HD), BF16),
            pltpu.VMEM((HEADS, 2, CHIP, HD), BF16),
            pltpu.VMEM((HEADS, 2, CHIP, HD), BF16),
            pltpu.VMEM((HEADS, 2, 2, TOK, HD), BF16),
            pltpu.VMEM((HEADS, 2, TOK, HD), BF16),
            pltpu.VMEM((HEADS, 2, TOK, HD), BF16),
            pltpu.VMEM((HEADS, 2, 2, TOK, HD), F32),
            pltpu.VMEM((TOK, half), BF16),
            dma((HEADS, 2, 2)),
            dma((HEADS, 2, 2)),
            dma((HEADS, 2)),
            dma((HEADS, 2)),
            dma((HEADS, 2)),
            dma((HEADS, 2)),
            dma((HEADS, 2, 2)),
            dma((HEADS, 2, 2)),
            dma((HEADS, 2)),
            dma((HEADS, 2)),
            dma((4,)),
            dma((4,)),
            dma((HEADS,)),
            dma((HEADS,)),
            dma((4,)),
            dma((4,)),
            dma((dp_size,)),
            dma((dp_size,)),
            dma((lax.axis_size("tensor") // 2 - 1,)),
            dma,
            dma((2, 2)),
            dma((2, 2)),
            dma((2,)),
            dma((2,)),
            dma,
            dma,
        ],
        compiler_params=pltpu.CompilerParams(
            collective_id=0, has_side_effects=True, vmem_limit_bytes=60 * 1024 * 1024
        ),
        cost_estimate=pl.CostEstimate(flops=2_000_000_000, bytes_accessed=4_000_000, transcendentals=4_000_000),
    )(
        import_row(reward),
        import_row(group_id),
        import_row(keep),
        import_row(dest),
        doc_len,
        *[pltpu.with_memory_space_constraint(a, pltpu.HBM) for a in (query, key, value, grad_out)],
    )
    return pl.pallas_call(
        hand_over,
        out_shape=shapes,
        in_specs=[pl.BlockSpec(memory_space=pltpu.VMEM)] * 3,
        out_specs=[hbm] * 3,
        scratch_shapes=[dma((3,))],
        compiler_params=pltpu.CompilerParams(vmem_limit_bytes=4 * 1024 * 1024),
    )(*[pltpu.with_memory_space_constraint(a, pltpu.VMEM) for a in results])


def solution(mesh):
    return jax.shard_map(
        body,
        mesh=mesh,
        in_specs=(
            P("dp"),
            P("dp"),
            P("dp"),
            P("dp"),
            P("dp", None),
            P(("dp", "tensor"), None),
            P(("dp", "tensor"), None),
            P(("dp", "tensor"), None),
            P(("dp", "tensor"), None),
        ),
        out_specs=(P(("dp", "tensor"), None), P(("dp", "tensor"), None), P(("dp", "tensor"), None)),
        check_vma=False,
    )
```
